256 devices in a mesh: table: 8 (over y, core), dp: 32 (over z, x).
Axes of the slice: x: 4, y: 4, z: 8, core: 2. Of those that a mesh axis runs over, the one named last changes fastest.
Arguments:
- hot_table: bfloat16 [512, 1024], replicated, may hold values from -6 to 6
- cold_table: bfloat16 [4096, 1024], P('table'), may hold values from -6 to 6
- w_in: bfloat16 [1024, 2048], replicated, may hold values from -0.1875 to 0.1875
- w_out: bfloat16 [512, 1024], replicated, may hold values from -0.25 to 0.25
- seq_lengths: int32 [256, 8], P(('table', 'dp')), may hold values from 1 to 256, 512 in all within a row
- event_hot: int32 [131072], P(('table', 'dp')), may hold values from 0 to 1
- event_index: int32 [131072], P(('table', 'dp')), may hold values from 0 to 511, as said below
- cold_requests: int32 [2048, 16], P(('table', 'dp')), may hold values from 0 to 511, as said below
- out_grad: bfloat16 [131072, 1024], P(('table', 'dp')), may hold values from -6 to 6
Outputs:
- layer_out: bfloat16 [131072, 1024], P(('table', 'dp'))
- hot_grad: float32 [512, 1024], P('dp')
- cold_grad: float32 [4096, 1024], P(('table', 'dp'))
The draws below stay inside these ranges and needn't reach their ends.
Inputs may be any that keep to these rules, and one draw needn't show every extreme that they name: `event_index`: where event_hot is 1 the value is a row of hot_table, below 512; where it is 0 it is a slot of the event's device, below 128. `cold_requests`: the 16 entries of one row are distinct.
All inputs are finite; a program needn't handle non-finite values.
Results may differ from the reference program's by a relative error of at most 0.012.
Values may be sent and summed in bfloat16 or wider, within the bound.
No kernel may reach another device: no remote copies, remote signals or barrier semaphores. Data moves between devices by JAX's collectives and lax.ppermute only.
A program may use at most 128 MiB of HBM per device.

```python
import math
import jax
import jax.numpy as jnp
import numpy as np
from jax import lax

D = 1024
HEADS = 4
HEAD = 128
TOK_DEV = 512
NSEQ = 8
HOT = 512
ROWS_SHARD = 512
CAP = 16
MOST = 256
TOKENS = 131072
COLD = 4096
N_TABLE = 8
N_DP = 32


def event_flags(key):
    flag_key = jax.random.fold_in(key, 11)
    return jax.random.randint(flag_key, (TOKENS,), 0, 2).astype(jnp.int32)


def draw_event_hot(key, part):
    return event_flags(key)


def draw_event_index(key, part):
    flags = event_flags(key)
    key = jax.random.fold_in(key, 5)
    first, second = jax.random.split(key)
    hot_pick = jax.random.randint(first, (TOKENS,), 0, HOT)
    cold_pick = jax.random.randint(second, (TOKENS,), 0, N_TABLE * CAP)
    return jnp.where(flags == 1, hot_pick, cold_pick).astype(jnp.int32)


def draw_cold_requests(key, part):
    key = jax.random.fold_in(key, 7)
    row_count = N_TABLE * N_DP * N_TABLE
    ranks = jax.random.randint(key, (row_count, ROWS_SHARD), 0, 4096)
    scores = ranks * ROWS_SHARD + lax.iota(jnp.int32, ROWS_SHARD)[None, :]
    order = jnp.argsort(scores, axis=1, stable=True)
    return order[:, :CAP].astype(jnp.int32)


def level_of(key, shape, shards, least, high):
    loudness = 1.0
    for axis_at, blocks in shards:
        heights = jax.random.uniform(jax.random.fold_in(jax.random.fold_in(key, 6), axis_at), (blocks,), jnp.float32, least / len(shards), high / len(shards))
        loudness = loudness * jnp.repeat(jnp.exp(heights), shape[axis_at] // blocks).reshape((-1,) + (1,) * (len(shape) - 1 - axis_at))
    return loudness


def length_profile(number_of, total, reach, skew):
    portions = [(1 << 20) // math.isqrt(grade ** skew) + 1 for grade in range(2, number_of + 1)]
    spare, given = total - reach - (number_of - 1), [1] * (number_of - 1)
    while spare > 0:
        candidates = [i for i in range(number_of - 1) if given[i] < reach]
        whole, remaining = sum([portions[i] for i in candidates]), spare
        for i in candidates:
            addition = min(reach - given[i], max(1, remaining * portions[i] // whole), spare)
            given[i] = given[i] + addition
            spare = spare - addition
    return np.array([reach] + given)


def uneven(own_key, amount, total, limit, lean):
    if amount == 2:
        one = jax.random.randint(own_key, (), max(1, total - limit), min(limit, total - 1) + 1)
        return jnp.stack([one, total - one])
    tallies = jnp.asarray(length_profile(amount, total, limit, lean), jnp.int32)
    twos = (amount - 1) // 2
    source_of, receiver = tallies[1:1 + 2 * twos:2], tallies[2:2 + 2 * twos:2]
    slack = jnp.minimum(source_of - 1, limit - receiver)
    passed = jax.random.randint(jax.random.fold_in(own_key, 1), (twos,), 0, 1 << 20) % (slack + 1)
    tallies = tallies.at[1:1 + 2 * twos:2].set(source_of - passed).at[2:2 + 2 * twos:2].set(receiver + passed)
    return tallies[jax.random.permutation(jax.random.fold_in(own_key, 2), amount)]


def centred(own_key, dims, width, most, cuts=(), dtype=jnp.bfloat16):
    loudness = level_of(own_key, dims, cuts, -0.22, 0.18) if cuts else 1.0
    drawn = jax.random.normal(own_key, dims, jnp.float32) * width * loudness
    return jnp.minimum(jnp.maximum(drawn, -most), most).astype(dtype)


def setup_inputs(seed: int = 0) -> dict:
    keys = jax.random.split(jax.random.key(seed), 10)
    hot_table = centred(keys[0], (HOT, D), 1.0, 6.0)
    cold_table = centred(keys[1], (COLD, D), 1.0, 6.0, ((0, 8),))
    w_in = centred(keys[2], (D, 4 * HEADS * HEAD), D ** -0.5, 0.1875)
    w_out = centred(keys[3], (HEADS * HEAD, D), (HEADS * HEAD) ** -0.5, 0.25)
    seq_lengths = jax.vmap(lambda own: uneven(own, NSEQ, TOK_DEV, MOST, 2))(jax.random.split(keys[4], (N_TABLE * N_DP))).reshape((N_TABLE * N_DP, NSEQ)).astype(jnp.int32)
    event_hot = draw_event_hot(jax.random.fold_in(keys[9], 71), 0)
    event_index = draw_event_index(jax.random.fold_in(keys[9], 71), 0)
    cold_requests = draw_cold_requests(jax.random.fold_in(keys[9], 71), 0)
    out_grad = centred(keys[8], (TOKENS, D), 1.0, 6.0, ((0, 256),))
    return {"hot_table": hot_table, "cold_table": cold_table, "w_in": w_in, "w_out": w_out, "seq_lengths": seq_lengths, "event_hot": event_hot, "event_index": event_index, "cold_requests": cold_requests, "out_grad": out_grad}


eps = 1e-06

def layer_norm(values):
    average = lax.optimization_barrier(jnp.mean(values, axis=-1, keepdims=True))
    centered = values - average
    variance = lax.optimization_barrier(jnp.mean(centered * centered, axis=-1, keepdims=True))
    return centered * lax.rsqrt(variance + eps)

def causal_scale(lengths, tokens):
    seq_ends = jnp.cumsum(lengths)
    position = lax.iota(jnp.int32, tokens)
    seq_of = lax.optimization_barrier(jnp.sum((position[:, None] >= seq_ends[None, :]).astype(jnp.int32), axis=1))
    picks = seq_of[:, None] == lax.iota(jnp.int32, lengths.shape[0])[None, :]
    length_of = lax.optimization_barrier(jnp.sum(jnp.where(picks, lengths[None, :], 0), axis=1)).astype(jnp.float32)
    allowed = (seq_of[:, None] == seq_of[None, :]) & (position[:, None] >= position[None, :])
    return jnp.where(allowed, 1.0 / length_of[:, None], 0.0).astype(jnp.float32)

def layer_forward(row_vals, w_in, w_out, scale_rows):
    tokens = row_vals.shape[0]
    inner_width = w_out.shape[0]
    head_count = inner_width // HEAD
    normed = layer_norm(row_vals).astype(jnp.bfloat16)
    mixed = jax.nn.silu(jnp.dot(normed, w_in, preferred_element_type=jnp.float32)).astype(jnp.bfloat16)
    gate_vals = mixed[:, :inner_width].astype(jnp.float32)
    value_vals = mixed[:, inner_width:2 * inner_width].reshape(tokens, head_count, HEAD)
    query_vals = mixed[:, 2 * inner_width:3 * inner_width].reshape(tokens, head_count, HEAD)
    key_vals = mixed[:, 3 * inner_width:].reshape(tokens, head_count, HEAD)
    scores = jnp.einsum('qhd,khd->hqk', query_vals.astype(jnp.float32), key_vals.astype(jnp.float32)) * HEAD ** (-0.5)
    weights = (jax.nn.silu(scores) * scale_rows[None]).astype(jnp.bfloat16)
    attended = jnp.einsum('hqk,khd->qhd', weights.astype(jnp.float32), value_vals.astype(jnp.float32))
    attended = attended.reshape(tokens, inner_width)
    merged = (layer_norm(attended) * gate_vals).astype(jnp.bfloat16)
    return jnp.dot(merged, w_out, preferred_element_type=jnp.float32) + row_vals

def reference(hot_table, cold_table, w_in, w_out, seq_lengths, event_hot, event_index, cold_requests, out_grad):
    devices = N_TABLE * N_DP
    slot_count = N_TABLE * CAP
    flags_all = event_hot.reshape(devices, TOK_DEV)
    index_all = event_index.reshape(devices, TOK_DEV)
    requests_all = cold_requests.reshape(devices, N_TABLE, CAP)
    grads_all = out_grad.reshape(devices, TOK_DEV, D)
    owners = lax.iota(jnp.int32, N_TABLE)[:, None] * ROWS_SHARD

    def visit(carry, item):
        hot_sum, cold_sum = carry
        lengths, hot_flags, row_index, requests, grad_rows = item
        global_rows = (owners + requests).reshape(slot_count).astype(jnp.int32)
        fetched = cold_table[global_rows]
        is_hot = hot_flags == 1
        hot_index = jnp.where(is_hot, row_index, 0).astype(jnp.int32)
        cold_index = jnp.where(is_hot, 0, row_index).astype(jnp.int32)
        row_vals = jnp.where(is_hot[:, None], hot_table[hot_index], fetched[cold_index]).astype(jnp.float32)
        scale_rows = causal_scale(lengths, TOK_DEV)
        pre_out, pullback = jax.vjp(lambda inputs: layer_forward(inputs, w_in, w_out, scale_rows), row_vals)
        row_grads = pullback(grad_rows.astype(jnp.float32))[0]
        hot_part = jax.ops.segment_sum(jnp.where(is_hot[:, None], row_grads, 0.0), hot_index, num_segments=HOT)
        slot_part = jax.ops.segment_sum(jnp.where(is_hot[:, None], 0.0, row_grads), cold_index, num_segments=slot_count)
        cold_sum = cold_sum.at[global_rows].add(slot_part)
        return ((hot_sum + hot_part, cold_sum), pre_out.astype(jnp.bfloat16))
    start = (jnp.zeros((HOT, D), jnp.float32), jnp.zeros((N_TABLE * ROWS_SHARD, D), jnp.float32))
    totals, outputs = lax.scan(visit, start, (seq_lengths, flags_all, index_all, requests_all, grads_all))
    return (outputs.reshape(devices * TOK_DEV, D), totals[0], totals[1])
```

```python
import jax
import jax.numpy as jnp
from jax import lax
from jax.sharding import PartitionSpec as P

HEAD = 128


eps = 1e-06


def layer_norm(values):
    average = jnp.mean(values, axis=-1, keepdims=True)
    centered = values - average
    variance = jnp.mean(centered * centered, axis=-1, keepdims=True)
    return centered * lax.rsqrt(variance + eps)


def causal_scale(lengths, tokens):
    seq_ends = jnp.cumsum(lengths)
    position = lax.iota(jnp.int32, tokens)
    seq_of = jnp.sum((position[:, None] >= seq_ends[None, :]).astype(jnp.int32), axis=1)
    picks = seq_of[:, None] == lax.iota(jnp.int32, lengths.shape[0])[None, :]
    length_of = jnp.sum(jnp.where(picks, lengths[None, :], 0), axis=1).astype(jnp.float32)
    allowed = (seq_of[:, None] == seq_of[None, :]) & (position[:, None] >= position[None, :])
    return jnp.where(allowed, 1.0 / length_of[:, None], 0.0)


def layer_forward(row_vals, w_in, w_out, scale_rows):
    tokens = row_vals.shape[0]
    inner_width = w_out.shape[0]
    head_count = inner_width // HEAD
    normed = layer_norm(row_vals).astype(jnp.bfloat16)
    mixed = jax.nn.silu(jnp.dot(normed, w_in, preferred_element_type=jnp.float32)).astype(
        jnp.bfloat16
    )
    gate_vals = mixed[:, :inner_width].astype(jnp.float32)
    value_vals = mixed[:, inner_width : 2 * inner_width].reshape(tokens, head_count, HEAD)
    query_vals = mixed[:, 2 * inner_width : 3 * inner_width].reshape(tokens, head_count, HEAD)
    key_vals = mixed[:, 3 * inner_width :].reshape(tokens, head_count, HEAD)
    scores = jnp.einsum(
        "qhd,khd->hqk", query_vals, key_vals, preferred_element_type=jnp.float32
    ) * HEAD ** (-0.5)
    weights = (jax.nn.silu(scores) * scale_rows[None]).astype(jnp.bfloat16)
    attended = jnp.einsum("hqk,khd->qhd", weights, value_vals, preferred_element_type=jnp.float32)
    attended = attended.reshape(tokens, inner_width)
    merged = (layer_norm(attended) * gate_vals).astype(jnp.bfloat16)
    return jnp.dot(merged, w_out, preferred_element_type=jnp.float32) + row_vals


def shift(groups, step):
    return [(g[i], g[(i + step) % len(g)]) for g in groups for i in range(len(g))]


CORE_GROUPS = [[2 * y, 2 * y + 1] for y in range(4)]
Y_GROUPS = [[2 * y + core for y in range(4)] for core in range(2)]
X_GROUPS = [[4 * z + x for x in range(4)] for z in range(8)]
Z_GROUPS = [[4 * z + x for z in range(8)] for x in range(4)]


def reduce_stage(chunks, axis, groups):
    total = chunks[0].astype(jnp.float32)
    arrived = [
        lax.ppermute(chunk, axis, shift(groups, k)) for k, chunk in enumerate(chunks) if k > 0
    ]
    for piece in arrived:
        total = total + piece.astype(jnp.float32)
    return total.astype(jnp.bfloat16)


def one_hot_rows(ids, rows):
    return (lax.iota(jnp.int32, rows)[:, None] == ids[None, :]).astype(jnp.bfloat16)


def on_device(
    hot_table, cold_table, w_in, w_out, seq_lengths, event_hot, event_index, cold_requests, out_grad
):
    table_count = lax.axis_size("table")
    cap_size = cold_requests.shape[1]
    slot_count = table_count * cap_size
    shard_rows = cold_table.shape[0]
    model_width = cold_table.shape[1]
    hot_rows = hot_table.shape[0]
    table_at, dp_at = lax.axis_index("table"), lax.axis_index("dp")
    y_at, core_at, x_at = table_at // 2, table_at % 2, dp_at % 4

    wanted = lax.all_to_all(cold_requests, "table", split_axis=0, concat_axis=0, tiled=True)
    wanted = wanted.reshape(slot_count)
    fetched = lax.all_to_all(
        cold_table[wanted].reshape(table_count, cap_size, model_width),
        "table",
        split_axis=0,
        concat_axis=0,
        tiled=True,
    ).reshape(slot_count, model_width)
    is_hot = event_hot == 1
    hot_index = jnp.where(is_hot, event_index, 0)
    cold_index = jnp.where(is_hot, 0, event_index)
    row_vals = jnp.where(is_hot[:, None], hot_table[hot_index], fetched[cold_index]).astype(
        jnp.float32
    )
    scale_rows = causal_scale(seq_lengths[0], row_vals.shape[0])
    pre_out, pullback = jax.vjp(
        lambda inputs: layer_forward(inputs, w_in, w_out, scale_rows), row_vals
    )
    row_grads = pullback(out_grad.astype(jnp.float32))[0].astype(jnp.bfloat16)

    hot_dp, hot_t = event_index // 16, (event_index % 16) // 2
    hot_place = (
        (hot_t % 2 - core_at) % 2 * 256
        + (hot_t // 2 - y_at) % 4 * 64
        + (hot_dp % 4 - x_at) % 4 * 16
        + hot_dp // 4 * 2
        + event_index % 2
    )
    hot_pick = one_hot_rows(jnp.where(is_hot, hot_place, -1), hot_rows)
    slot_pick = one_hot_rows(jnp.where(is_hot, -1, event_index), slot_count)
    slot_part = jnp.dot(slot_pick, row_grads, preferred_element_type=jnp.float32).astype(
        jnp.bfloat16
    )
    hot_part = jnp.dot(hot_pick, row_grads, preferred_element_type=jnp.float32).astype(jnp.bfloat16)
    hot_part = reduce_stage([hot_part[:256], hot_part[256:]], "table", CORE_GROUPS)
    returned = lax.all_to_all(
        slot_part.reshape(table_count, cap_size, model_width),
        "table",
        split_axis=0,
        concat_axis=0,
        tiled=True,
    ).reshape(slot_count, model_width)
    hot_part = reduce_stage([hot_part[64 * k : 64 * k + 64] for k in range(4)], "table", Y_GROUPS)
    shard_place = (wanted // 16 % 4 - x_at) % 4 * 128 + wanted // 64 * 16 + wanted % 16
    shard_pick = one_hot_rows(shard_place, shard_rows)
    shard_grad = jnp.dot(shard_pick, returned, preferred_element_type=jnp.float32).astype(
        jnp.bfloat16
    )
    both = [
        jnp.concatenate([shard_grad[128 * k : 128 * k + 128], hot_part[16 * k : 16 * k + 16]])
        for k in range(4)
    ]
    both = reduce_stage(both, "dp", X_GROUPS)
    by_z = jnp.concatenate(
        [both[:128].reshape(8, 16, model_width), both[128:].reshape(8, 2, model_width)], axis=1
    )
    by_z = lax.all_to_all(
        by_z, "dp", split_axis=0, concat_axis=0, tiled=True, axis_index_groups=Z_GROUPS
    )
    summed = jnp.sum(by_z.astype(jnp.float32), axis=0)
    hot_sum = lax.all_gather(summed[16:], "table", axis=0, tiled=True)
    return (pre_out.astype(jnp.bfloat16), hot_sum, summed[:16])


def solution(mesh):
    placed = (
        P(),
        P("table", None),
        P(),
        P(),
        P(("table", "dp"), None),
        P(("table", "dp")),
        P(("table", "dp")),
        P(("table", "dp"), None),
        P(("table", "dp"), None),
    )
    return jax.shard_map(
        on_device,
        mesh=mesh,
        in_specs=placed,
        out_specs=(P(("table", "dp"), None), P("dp", None), P(("table", "dp"), None)),
        check_vma=False,
    )
```

```python
import jax
import jax.numpy as jnp
from jax import lax
from jax.experimental import pallas as pl
from jax.experimental.pallas import tpu as pltpu
from jax.sharding import PartitionSpec as P

HEAD = 128


EPS = 1e-06
BLOCK = 128
BACK = 2


def sigmoid(values):
    return 0.5 * jnp.tanh(0.5 * values) + 0.5


def mean_of(values):
    return jnp.mean(values, axis=-1, keepdims=True)


def dot_nn(a, b):
    return jnp.dot(a, b, preferred_element_type=jnp.float32)


def dot_nt(a, b):
    return lax.dot_general(a, b, (((1,), (1,)), ((), ())), preferred_element_type=jnp.float32)


def dot_tn(a, b):
    return lax.dot_general(a, b, (((0,), (0,)), ((), ())), preferred_element_type=jnp.float32)


def layer_kernel(
    lengths_ref,
    hot_ref,
    fetched_ref,
    w_in_ref,
    w_out_ref,
    out_grad_ref,
    source_ref,
    place_ref,
    layer_out_ref,
    near_ref,
    far_ref,
    slots_ref,
    rows_ref,
    normed_ref,
    rstd_ref,
    mixed_ref,
    slope_ref,
    weights_ref,
    dscore_ref,
    attended_ref,
    dvalue_ref,
    dkey_ref,
    dpre_ref,
    dnorm_ref,
):
    tokens, width = rows_ref.shape
    hot_rows, slot_count = hot_ref.shape[0], fetched_ref.shape[0]
    inner = w_out_ref.shape[0]
    heads = inner // HEAD
    bf16, f32 = jnp.bfloat16, jnp.float32

    @pl.loop(0, tokens // BLOCK)
    def _(step):
        at = pl.ds(pl.multiple_of(step * BLOCK, BLOCK), BLOCK)
        source = source_ref[at, :]
        hot_pick = (source == lax.broadcasted_iota(jnp.int32, (BLOCK, hot_rows), 1)).astype(bf16)
        slot_pick = (
            source == lax.broadcasted_iota(jnp.int32, (BLOCK, slot_count), 1) + hot_rows
        ).astype(bf16)
        rows = dot_nn(hot_pick, hot_ref[...]) + dot_nn(slot_pick, fetched_ref[...])
        centered = rows - mean_of(rows)
        rstd = lax.rsqrt(mean_of(centered * centered) + EPS)
        rows_ref[at, :] = rows.astype(bf16)
        normed_ref[at, :] = (centered * rstd).astype(bf16)
        rstd_ref[at, :] = rstd

    @pl.loop(0, 4 * inner // 256)
    def _(step):
        at = pl.ds(pl.multiple_of(step * 256, 256), 256)
        pre = dot_nn(normed_ref[...], w_in_ref[:, at])
        sig = sigmoid(pre)
        act = pre * sig
        mixed_ref[:, at] = act.astype(bf16)
        slope_ref[:, at] = (sig + act * (1.0 - sig)).astype(bf16)

    def columns(part, head):
        return pl.ds(part * inner + head * HEAD, HEAD)

    for block in range(tokens // BLOCK):
        q_at = pl.ds(block * BLOCK, BLOCK)
        first = max(0, block - BACK)
        reach = (block + 1 - first) * BLOCK
        k_at = pl.ds(first * BLOCK, reach)
        position = lax.broadcasted_iota(jnp.int32, (BLOCK, 1), 0) + block * BLOCK
        begin = jnp.zeros((BLOCK, 1), jnp.int32)
        length = jnp.zeros((BLOCK, 1), jnp.int32)
        end = jnp.int32(0)
        for history in range(lengths_ref.shape[1]):
            start = end
            end = start + lengths_ref[0, history]
            inside = position >= start
            begin = jnp.where(inside, start, begin)
            length = jnp.where(inside, end - start, length)
        key_position = lax.broadcasted_iota(jnp.int32, (BLOCK, reach), 1) + first * BLOCK
        allowed = (key_position <= position) & (key_position >= begin)
        share = jnp.where(allowed, 1.0 / length.astype(f32), 0.0)
        for head in range(heads):
            scores = dot_nt(
                mixed_ref[q_at, columns(2, head)], mixed_ref[k_at, columns(3, head)]
            ) * (HEAD ** -0.5)
            sig = sigmoid(scores)
            act = scores * sig
            weights = (act * share).astype(bf16)
            weights_ref[head, q_at, :reach] = weights
            dscore_ref[head, q_at, :reach] = (
                (sig + act * (1.0 - sig)) * (share * (HEAD ** -0.5))
            ).astype(bf16)
            attended_ref[q_at, pl.ds(head * HEAD, HEAD)] = dot_nn(
                weights, mixed_ref[k_at, columns(1, head)]
            )

    for block in range(tokens // 256):
        at = pl.ds(block * 256, 256)
        attended = attended_ref[at, :]
        centered = attended - mean_of(attended)
        rstd = lax.rsqrt(mean_of(centered * centered) + EPS)
        unit = centered * rstd
        gate = mixed_ref[at, :inner].astype(f32)
        merged = (unit * gate).astype(bf16)
        layer_out_ref[at, :] = (
            dot_nn(merged, w_out_ref[...]) + rows_ref[at, :].astype(f32)
        ).astype(bf16)
        dmerged = dot_nt(out_grad_ref[at, :], w_out_ref[...])
        dpre_ref[at, :inner] = (dmerged * unit * slope_ref[at, :inner].astype(f32)).astype(bf16)
        dunit = dmerged * gate
        attended_ref[at, :] = rstd * (dunit - mean_of(dunit) - unit * mean_of(dunit * unit))

    dvalue_ref[...] = jnp.zeros_like(dvalue_ref)
    dkey_ref[...] = jnp.zeros_like(dkey_ref)
    for block in range(tokens // BLOCK):
        q_at = pl.ds(block * BLOCK, BLOCK)
        first = max(0, block - BACK)
        reach = (block + 1 - first) * BLOCK
        k_at = pl.ds(first * BLOCK, reach)
        for head in range(heads):
            own = pl.ds(head * HEAD, HEAD)
            dattended = attended_ref[q_at, own].astype(bf16)
            dweights = dot_nt(dattended, mixed_ref[k_at, columns(1, head)])
            dscores = (dweights * dscore_ref[head, q_at, :reach].astype(f32)).astype(bf16)
            dquery = dot_nn(dscores, mixed_ref[k_at, columns(3, head)])
            dpre_ref[q_at, columns(2, head)] = (
                dquery * slope_ref[q_at, columns(2, head)].astype(f32)
            ).astype(bf16)
            dvalue_ref[k_at, own] += dot_tn(weights_ref[head, q_at, :reach], dattended)
            dkey_ref[k_at, own] += dot_tn(dscores, mixed_ref[q_at, columns(2, head)])
    values, keys = pl.ds(inner, inner), pl.ds(3 * inner, inner)
    dpre_ref[:, values] = (dvalue_ref[...] * slope_ref[:, values].astype(f32)).astype(bf16)
    dpre_ref[:, keys] = (dkey_ref[...] * slope_ref[:, keys].astype(f32)).astype(bf16)

    @pl.loop(0, width // 256)
    def _(step):
        at = pl.ds(pl.multiple_of(step * 256, 256), 256)
        dnorm_ref[:, at] = dot_nt(dpre_ref[...], w_in_ref[at, :])

    @pl.loop(0, tokens // BLOCK)
    def _(step):
        at = pl.ds(pl.multiple_of(step * BLOCK, BLOCK), BLOCK)
        rows = rows_ref[at, :].astype(f32)
        rstd = rstd_ref[at, :]
        unit = (rows - mean_of(rows)) * rstd
        dunit = dnorm_ref[at, :]
        grads = rstd * (dunit - mean_of(dunit) - unit * mean_of(dunit * unit))
        normed_ref[at, :] = (grads + out_grad_ref[at, :].astype(f32)).astype(bf16)

    base = 0
    for ref in (near_ref, far_ref, slots_ref):
        count = ref.shape[0]
        pick = (
            lax.broadcasted_iota(jnp.int32, (count, tokens), 0) + base == place_ref[...]
        ).astype(bf16)
        base += count
        for half in range(2):
            at = pl.ds(half * (width // 2), width // 2)
            ref[:, at] = dot_nn(pick, normed_ref[:, at]).astype(bf16)


def layer(lengths, hot_table, fetched, w_in, w_out, out_grad, source, place):
    tokens, width = out_grad.shape
    inner = w_out.shape[0]
    heads = inner // HEAD
    half = hot_table.shape[0] // 2
    bf16, f32 = jnp.bfloat16, jnp.float32
    vmem = pl.BlockSpec(memory_space=pltpu.VMEM)
    reach = (BACK + 1) * BLOCK
    return pl.pallas_call(
        layer_kernel,
        out_shape=(
            jax.ShapeDtypeStruct((tokens, width), bf16),
            jax.ShapeDtypeStruct((half, width), bf16),
            jax.ShapeDtypeStruct((half, width), bf16),
            jax.ShapeDtypeStruct(fetched.shape, bf16),
        ),
        in_specs=[pl.BlockSpec(memory_space=pltpu.SMEM)] + [vmem] * 7,
        out_specs=(vmem,) * 4,
        scratch_shapes=[
            pltpu.VMEM((tokens, width), bf16),
            pltpu.VMEM((tokens, width), bf16),
            pltpu.VMEM((tokens, 1), f32),
            pltpu.VMEM((tokens, 4 * inner), bf16),
            pltpu.VMEM((tokens, 4 * inner), bf16),
            pltpu.VMEM((heads, tokens, reach), bf16),
            pltpu.VMEM((heads, tokens, reach), bf16),
            pltpu.VMEM((tokens, inner), f32),
            pltpu.VMEM((tokens, inner), f32),
            pltpu.VMEM((tokens, inner), f32),
            pltpu.VMEM((tokens, 4 * inner), bf16),
            pltpu.VMEM((tokens, width), f32),
        ],
        compiler_params=pltpu.CompilerParams(vmem_limit_bytes=48 * 1024 * 1024),
        cost_estimate=pl.CostEstimate(flops=8 * 10**9, bytes_accessed=12 * 10**6, transcendentals=0),
        name="layer",
    )(lengths, hot_table, fetched, w_in, w_out, out_grad, source, place)


def shift(groups, step):
    return [(g[i], g[(i + step) % len(g)]) for g in groups for i in range(len(g))]


CORE_GROUPS = [[2 * y, 2 * y + 1] for y in range(4)]
Y_GROUPS = [[2 * y + core for y in range(4)] for core in range(2)]
X_GROUPS = [[4 * z + x for x in range(4)] for z in range(8)]
Z_GROUPS = [[4 * z + x for z in range(8)] for x in range(4)]


def reduce_stage(chunks, axis, groups):
    total = chunks[0].astype(jnp.float32)
    arrived = [
        lax.ppermute(chunk, axis, shift(groups, k)) for k, chunk in enumerate(chunks) if k > 0
    ]
    for piece in arrived:
        total = total + piece.astype(jnp.float32)
    return total.astype(jnp.bfloat16)


def one_hot_rows(ids, rows):
    return (lax.iota(jnp.int32, rows)[:, None] == ids[None, :]).astype(jnp.bfloat16)


def on_device(
    hot_table, cold_table, w_in, w_out, seq_lengths, event_hot, event_index, cold_requests, out_grad
):
    table_count = lax.axis_size("table")
    cap_size = cold_requests.shape[1]
    slot_count = table_count * cap_size
    shard_rows = cold_table.shape[0]
    model_width = cold_table.shape[1]
    hot_rows = hot_table.shape[0]
    table_at, dp_at = lax.axis_index("table"), lax.axis_index("dp")
    y_at, core_at, x_at = table_at // 2, table_at % 2, dp_at % 4

    wanted = lax.all_to_all(cold_requests, "table", split_axis=0, concat_axis=0, tiled=True)
    wanted = wanted.reshape(slot_count)
    fetched = lax.all_to_all(
        cold_table[wanted].reshape(table_count, cap_size, model_width),
        "table",
        split_axis=0,
        concat_axis=0,
        tiled=True,
    ).reshape(slot_count, model_width)
    is_hot = event_hot == 1
    hot_dp, hot_t = event_index // 16, (event_index % 16) // 2
    hot_place = (
        (hot_t % 2 - core_at) % 2 * 256
        + (hot_t // 2 - y_at) % 4 * 64
        + (hot_dp % 4 - x_at) % 4 * 16
        + hot_dp // 4 * 2
        + event_index % 2
    )
    source = jnp.where(is_hot, event_index, event_index + hot_rows)
    place = jnp.where(is_hot, hot_place, event_index + hot_rows)
    layer_out, near_part, far_part, slot_part = layer(
        seq_lengths,
        hot_table,
        fetched,
        w_in,
        w_out,
        out_grad,
        source.reshape(-1, 1),
        place.reshape(1, -1),
    )
    hot_part = reduce_stage([near_part, far_part], "table", CORE_GROUPS)
    returned = lax.all_to_all(
        slot_part.reshape(table_count, cap_size, model_width),
        "table",
        split_axis=0,
        concat_axis=0,
        tiled=True,
    ).reshape(slot_count, model_width)
    hot_part = reduce_stage([hot_part[64 * k : 64 * k + 64] for k in range(4)], "table", Y_GROUPS)
    shard_place = (wanted // 16 % 4 - x_at) % 4 * 128 + wanted // 64 * 16 + wanted % 16
    shard_pick = one_hot_rows(shard_place, shard_rows)
    shard_grad = jnp.dot(shard_pick, returned, preferred_element_type=jnp.float32).astype(
        jnp.bfloat16
    )
    both = [
        jnp.concatenate([shard_grad[128 * k : 128 * k + 128], hot_part[16 * k : 16 * k + 16]])
        for k in range(4)
    ]
    both = reduce_stage(both, "dp", X_GROUPS)
    by_z = jnp.concatenate(
        [both[:128].reshape(8, 16, model_width), both[128:].reshape(8, 2, model_width)], axis=1
    )
    by_z = lax.all_to_all(
        by_z, "dp", split_axis=0, concat_axis=0, tiled=True, axis_index_groups=Z_GROUPS
    )
    summed = jnp.sum(by_z.astype(jnp.float32), axis=0)
    hot_sum = lax.all_gather(summed[16:], "table", axis=0, tiled=True)
    return (layer_out, hot_sum, summed[:16])


def solution(mesh):
    placed = (
        P(),
        P("table", None),
        P(),
        P(),
        P(("table", "dp"), None),
        P(("table", "dp")),
        P(("table", "dp")),
        P(("table", "dp"), None),
        P(("table", "dp"), None),
    )
    return jax.shard_map(
        on_device,
        mesh=mesh,
        in_specs=placed,
        out_specs=(P(("table", "dp"), None), P("dp", None), P(("table", "dp"), None)),
        check_vma=False,
    )
```

```python
import jax
import jax.numpy as jnp
from jax import lax
from jax.experimental import pallas as pl
from jax.experimental.pallas import tpu as pltpu
from jax.sharding import PartitionSpec as P

HEAD = 128


EPS = 1e-06
BLOCK = 128
BACK = 2


def sigmoid(values):
    return 0.5 * jnp.tanh(0.5 * values) + 0.5


def mean_of(values):
    return jnp.mean(values, axis=-1, keepdims=True)


def dot_nn(a, b):
    return jnp.dot(a, b, preferred_element_type=jnp.float32)


def dot_nt(a, b):
    return lax.dot_general(a, b, (((1,), (1,)), ((), ())), preferred_element_type=jnp.float32)


def dot_tn(a, b):
    return lax.dot_general(a, b, (((0,), (0,)), ((), ())), preferred_element_type=jnp.float32)


def pick_kernel(wanted_ref, table_ref, rows_ref):
    takers, cap = wanted_ref.shape
    shard_rows, count = table_ref.shape[0], takers * cap
    wide = jnp.concatenate([wanted_ref[...]] * takers, axis=1)
    taker = lax.broadcasted_iota(jnp.int32, (takers, count), 0)
    lane = lax.broadcasted_iota(jnp.int32, (takers, count), 1)
    own = (lane >= taker * cap) & (lane < taker * cap + cap)
    flat = jnp.sum(jnp.where(own, wide, 0), axis=0, keepdims=True)
    pick = (lax.broadcasted_iota(jnp.int32, (shard_rows, count), 0) == flat).astype(jnp.bfloat16)
    rows_ref[...] = dot_tn(pick, table_ref[...]).astype(jnp.bfloat16)


def pick_rows(wanted, table):
    vmem = pl.BlockSpec(memory_space=pltpu.VMEM)
    return pl.pallas_call(
        pick_kernel,
        out_shape=jax.ShapeDtypeStruct((wanted.size, table.shape[1]), jnp.bfloat16),
        in_specs=[vmem] * 2,
        out_specs=vmem,
        compiler_params=pltpu.CompilerParams(vmem_limit_bytes=4 * 1024 * 1024),
        name="pick_rows",
    )(wanted, table)


def layer_kernel(
    lengths_ref,
    fetched_ref,
    source_ref,
    place_ref,
    hot_hbm,
    w_in_hbm,
    w_out_hbm,
    out_grad_hbm,
    layer_out_hbm,
    near_ref,
    far_ref,
    hot_ref,
    w_in_ref,
    w_out_ref,
    out_grad_ref,
    layer_out_ref,
    rows_ref,
    normed_ref,
    rstd_ref,
    mixed_ref,
    slope_ref,
    weights_ref,
    dscore_ref,
    attended_ref,
    dvalue_ref,
    dkey_ref,
    dpre_ref,
    dnorm_ref,
    sems,
):
    tokens, width = rows_ref.shape
    hot_rows, slot_count = hot_ref.shape[0], fetched_ref.shape[0]
    inner = w_out_ref.shape[0]
    heads = inner // HEAD
    bf16, f32 = jnp.bfloat16, jnp.float32

    hot_copy = pltpu.make_async_copy(hot_hbm, hot_ref, sems.at[0])
    w_in_copy = pltpu.make_async_copy(w_in_hbm, w_in_ref, sems.at[1])
    w_out_copy = pltpu.make_async_copy(w_out_hbm, w_out_ref, sems.at[2])
    out_grad_copy = pltpu.make_async_copy(out_grad_hbm, out_grad_ref, sems.at[3])
    layer_out_copy = pltpu.make_async_copy(layer_out_ref, layer_out_hbm, sems.at[4])
    for copy in (hot_copy, w_in_copy, w_out_copy, out_grad_copy):
        copy.start()
    hot_copy.wait()

    @pl.loop(0, tokens // BLOCK)
    def _(step):
        at = pl.ds(pl.multiple_of(step * BLOCK, BLOCK), BLOCK)
        source = source_ref[at, :]
        hot_pick = (source == lax.broadcasted_iota(jnp.int32, (BLOCK, hot_rows), 1)).astype(bf16)
        slot_pick = (
            source == lax.broadcasted_iota(jnp.int32, (BLOCK, slot_count), 1) + hot_rows
        ).astype(bf16)
        rows = dot_nn(hot_pick, hot_ref[...]) + dot_nn(slot_pick, fetched_ref[...])
        centered = rows - mean_of(rows)
        rstd = lax.rsqrt(mean_of(centered * centered) + EPS)
        rows_ref[at, :] = rows.astype(bf16)
        normed_ref[at, :] = (centered * rstd).astype(bf16)
        rstd_ref[at, :] = rstd

    w_in_copy.wait()

    @pl.loop(0, 4 * inner // 256)
    def _(step):
        at = pl.ds(pl.multiple_of(step * 256, 256), 256)
        pre = dot_nn(normed_ref[...], w_in_ref[:, at])
        sig = sigmoid(pre)
        act = pre * sig
        mixed_ref[:, at] = act.astype(bf16)
        slope_ref[:, at] = (sig + act * (1.0 - sig)).astype(bf16)

    def columns(part, head):
        return pl.ds(part * inner + head * HEAD, HEAD)

    for block in range(tokens // BLOCK):
        q_at = pl.ds(block * BLOCK, BLOCK)
        first = max(0, block - BACK)
        reach = (block + 1 - first) * BLOCK
        k_at = pl.ds(first * BLOCK, reach)
        position = lax.broadcasted_iota(jnp.int32, (BLOCK, 1), 0) + block * BLOCK
        begin = jnp.zeros((BLOCK, 1), jnp.int32)
        length = jnp.zeros((BLOCK, 1), jnp.int32)
        end = jnp.int32(0)
        for history in range(lengths_ref.shape[1]):
            start = end
            end = start + lengths_ref[0, history]
            inside = position >= start
            begin = jnp.where(inside, start, begin)
            length = jnp.where(inside, end - start, length)
        key_position = lax.broadcasted_iota(jnp.int32, (BLOCK, reach), 1) + first * BLOCK
        allowed = (key_position <= position) & (key_position >= begin)
        share = jnp.where(allowed, 1.0 / length.astype(f32), 0.0)
        for head in range(heads):
            scores = dot_nt(
                mixed_ref[q_at, columns(2, head)], mixed_ref[k_at, columns(3, head)]
            ) * (HEAD ** -0.5)
            sig = sigmoid(scores)
            act = scores * sig
            weights = (act * share).astype(bf16)
            weights_ref[head, q_at, :reach] = weights
            dscore_ref[head, q_at, :reach] = (
                (sig + act * (1.0 - sig)) * (share * (HEAD ** -0.5))
            ).astype(bf16)
            attended_ref[q_at, pl.ds(head * HEAD, HEAD)] = dot_nn(
                weights, mixed_ref[k_at, columns(1, head)]
            )

    w_out_copy.wait()
    out_grad_copy.wait()

    for block in range(tokens // 256):
        at = pl.ds(block * 256, 256)
        attended = attended_ref[at, :]
        centered = attended - mean_of(attended)
        rstd = lax.rsqrt(mean_of(centered * centered) + EPS)
        unit = centered * rstd
        gate = mixed_ref[at, :inner].astype(f32)
        merged = (unit * gate).astype(bf16)
        layer_out_ref[at, :] = (
            dot_nn(merged, w_out_ref[...]) + rows_ref[at, :].astype(f32)
        ).astype(bf16)
        dmerged = dot_nt(out_grad_ref[at, :], w_out_ref[...])
        dpre_ref[at, :inner] = (dmerged * unit * slope_ref[at, :inner].astype(f32)).astype(bf16)
        dunit = dmerged * gate
        attended_ref[at, :] = rstd * (dunit - mean_of(dunit) - unit * mean_of(dunit * unit))

    layer_out_copy.start()

    dvalue_ref[...] = jnp.zeros_like(dvalue_ref)
    dkey_ref[...] = jnp.zeros_like(dkey_ref)
    for block in range(tokens // BLOCK):
        q_at = pl.ds(block * BLOCK, BLOCK)
        first = max(0, block - BACK)
        reach = (block + 1 - first) * BLOCK
        k_at = pl.ds(first * BLOCK, reach)
        for head in range(heads):
            own = pl.ds(head * HEAD, HEAD)
            dattended = attended_ref[q_at, own].astype(bf16)
            dweights = dot_nt(dattended, mixed_ref[k_at, columns(1, head)])
            dscores = (dweights * dscore_ref[head, q_at, :reach].astype(f32)).astype(bf16)
            dquery = dot_nn(dscores, mixed_ref[k_at, columns(3, head)])
            dpre_ref[q_at, columns(2, head)] = (
                dquery * slope_ref[q_at, columns(2, head)].astype(f32)
            ).astype(bf16)
            dvalue_ref[k_at, own] += dot_tn(weights_ref[head, q_at, :reach], dattended)
            dkey_ref[k_at, own] += dot_tn(dscores, mixed_ref[q_at, columns(2, head)])
    values, keys = pl.ds(inner, inner), pl.ds(3 * inner, inner)
    dpre_ref[:, values] = (dvalue_ref[...] * slope_ref[:, values].astype(f32)).astype(bf16)
    dpre_ref[:, keys] = (dkey_ref[...] * slope_ref[:, keys].astype(f32)).astype(bf16)

    @pl.loop(0, width // 256)
    def _(step):
        at = pl.ds(pl.multiple_of(step * 256, 256), 256)
        dnorm_ref[:, at] = dot_nt(dpre_ref[...], w_in_ref[at, :])

    @pl.loop(0, tokens // BLOCK)
    def _(step):
        at = pl.ds(pl.multiple_of(step * BLOCK, BLOCK), BLOCK)
        rstd = rstd_ref[at, :]
        unit = normed_ref[at, :].astype(f32)
        dunit = dnorm_ref[at, :]
        grads = rstd * (dunit - mean_of(dunit) - unit * mean_of(dunit * unit))
        normed_ref[at, :] = (grads + out_grad_ref[at, :].astype(f32)).astype(bf16)

    half = near_ref.shape[0]
    for base, ref in ((half, far_ref), (0, near_ref)):
        pick = (
            lax.broadcasted_iota(jnp.int32, (half, tokens), 0) + base == place_ref[...]
        ).astype(bf16)
        for part in range(2):
            at = pl.ds(part * (width // 2), width // 2)
            ref[:, at] = dot_nn(pick, normed_ref[:, at]).astype(bf16)
    layer_out_copy.wait()


def layer(lengths, hot_table, fetched, w_in, w_out, out_grad, source, place):
    tokens, width = out_grad.shape
    inner = w_out.shape[0]
    heads = inner // HEAD
    half = (hot_table.shape[0] + fetched.shape[0]) // 2
    bf16, f32 = jnp.bfloat16, jnp.float32
    vmem = pl.BlockSpec(memory_space=pltpu.VMEM)
    hbm = pl.BlockSpec(memory_space=pl.ANY)
    reach = (BACK + 1) * BLOCK
    return pl.pallas_call(
        layer_kernel,
        out_shape=(
            jax.ShapeDtypeStruct((tokens, width), bf16),
            jax.ShapeDtypeStruct((half, width), bf16),
            jax.ShapeDtypeStruct((half, width), bf16),
        ),
        in_specs=[pl.BlockSpec(memory_space=pltpu.SMEM)] + [vmem] * 3 + [hbm] * 4,
        out_specs=(hbm, vmem, vmem),
        scratch_shapes=[
            pltpu.VMEM(hot_table.shape, bf16),
            pltpu.VMEM(w_in.shape, bf16),
            pltpu.VMEM(w_out.shape, bf16),
            pltpu.VMEM((tokens, width), bf16),
            pltpu.VMEM((tokens, width), bf16),
            pltpu.VMEM((tokens, width), bf16),
            pltpu.VMEM((tokens, width), bf16),
            pltpu.VMEM((tokens, 1), f32),
            pltpu.VMEM((tokens, 4 * inner), bf16),
            pltpu.VMEM((tokens, 4 * inner), bf16),
            pltpu.VMEM((heads, tokens, reach), bf16),
            pltpu.VMEM((heads, tokens, reach), bf16),
            pltpu.VMEM((tokens, inner), f32),
            pltpu.VMEM((tokens, inner), f32),
            pltpu.VMEM((tokens, inner), f32),
            pltpu.VMEM((tokens, 4 * inner), bf16),
            pltpu.VMEM((tokens, width), f32),
            pltpu.SemaphoreType.DMA((5,)),
        ],
        compiler_params=pltpu.CompilerParams(vmem_limit_bytes=58 * 1024 * 1024),
        cost_estimate=pl.CostEstimate(flops=8 * 10**9, bytes_accessed=12 * 10**6, transcendentals=0),
        name="layer",
    )(lengths, fetched, source, place, hot_table, w_in, w_out, out_grad)


def core_sums_kernel(near_ref, got_ref, *out_refs):
    slots = near_ref.shape[0] // 5
    hot = near_ref.shape[0] - slots
    for k in range(4):
        piece = pl.ds(k * slots // 4 + hot, slots // 4)
        out_refs[k][: slots // 4, :] = near_ref[piece, :]
        out_refs[k][slots // 4 :, :] = got_ref[piece, :]
    for k in range(4):
        piece = pl.ds(k * hot // 4, hot // 4)
        total = near_ref[piece, :].astype(jnp.float32) + got_ref[piece, :].astype(jnp.float32)
        out_refs[4 + k][...] = total.astype(jnp.bfloat16)


def core_sums(near, got):
    size, width = near.shape[0] // 5, near.shape[1]
    vmem = pl.BlockSpec(memory_space=pltpu.VMEM)
    out = pl.pallas_call(
        core_sums_kernel,
        out_shape=[jax.ShapeDtypeStruct((size // 2, width), jnp.bfloat16)] * 4
        + [jax.ShapeDtypeStruct((size, width), jnp.bfloat16)] * 4,
        in_specs=[vmem] * 2,
        out_specs=[vmem] * 8,
        compiler_params=pltpu.CompilerParams(vmem_limit_bytes=8 * 1024 * 1024),
        name="core_sums",
    )(near, got)
    return out[:4], out[4:]


def shard_sums_kernel(place_ref, own_ref, first_ref, second_ref, third_ref, *out_refs):
    rows = out_refs[0].shape[0]
    slots = jnp.concatenate(
        [own_ref[...], first_ref[...], second_ref[...], third_ref[...]], axis=0
    )
    for k, ref in enumerate(out_refs):
        pick = (
            lax.broadcasted_iota(jnp.int32, (rows, slots.shape[0]), 0) + k * rows == place_ref[...]
        ).astype(jnp.bfloat16)
        ref[...] = dot_nn(pick, slots).astype(jnp.bfloat16)


def shard_sums(place, pieces, shard_rows):
    width = pieces[0].shape[1]
    vmem = pl.BlockSpec(memory_space=pltpu.VMEM)
    return pl.pallas_call(
        shard_sums_kernel,
        out_shape=[jax.ShapeDtypeStruct((shard_rows // 4, width), jnp.bfloat16)] * 4,
        in_specs=[vmem] * 5,
        out_specs=[vmem] * 4,
        compiler_params=pltpu.CompilerParams(vmem_limit_bytes=4 * 1024 * 1024),
        name="shard_sums",
    )(place, *pieces)


def shift(groups, step):
    return [(g[i], g[(i + step) % len(g)]) for g in groups for i in range(len(g))]


CORE_GROUPS = [[2 * y, 2 * y + 1] for y in range(4)]
Y_GROUPS = [[2 * y + core for y in range(4)] for core in range(2)]
X_GROUPS = [[4 * z + x for x in range(4)] for z in range(8)]
Z_GROUPS = [[4 * z + x for z in range(8)] for x in range(4)]


def exchange(chunks, axis, groups):
    return [
        chunk if k == 0 else lax.ppermute(chunk, axis, shift(groups, k))
        for k, chunk in enumerate(chunks)
    ]


def add_up(pieces):
    here, back_1, back_2, back_3 = [piece.astype(jnp.float32) for piece in pieces]
    return (here + back_2) + (back_1 + back_3)


def on_device(
    hot_table, cold_table, w_in, w_out, seq_lengths, event_hot, event_index, cold_requests, out_grad
):
    table_count = lax.axis_size("table")
    cap_size = cold_requests.shape[1]
    slot_count = table_count * cap_size
    shard_rows = cold_table.shape[0]
    model_width = cold_table.shape[1]
    hot_rows = hot_table.shape[0]
    table_at, dp_at = lax.axis_index("table"), lax.axis_index("dp")
    y_at, core_at, x_at = table_at // 2, table_at % 2, dp_at % 4

    wanted = lax.all_to_all(cold_requests, "table", split_axis=0, concat_axis=0, tiled=True)
    fetched = lax.all_to_all(
        pick_rows(wanted, cold_table).reshape(table_count, cap_size, model_width),
        "table",
        split_axis=0,
        concat_axis=0,
        tiled=True,
    ).reshape(slot_count, model_width)
    wanted = wanted.reshape(slot_count)
    is_hot = event_hot == 1

    hot_dp, hot_t = event_index // 16, (event_index % 16) // 2
    hot_place = (
        (hot_t % 2 - core_at) % 2 * 320
        + (hot_dp % 4 - x_at) % 4 * 64
        + hot_dp // 4 * 8
        + hot_t // 2 * 2
        + event_index % 2
    )
    slot_t = event_index // 16
    slot_place = (
        (slot_t % 2 - core_at) % 2 * 320
        + 256
        + (slot_t // 2 - y_at) % 4 * 16
        + event_index % 16
    )
    source = jnp.where(is_hot, event_index, event_index + hot_rows)
    place = jnp.where(is_hot, hot_place, slot_place)
    layer_out, near, far = layer(
        seq_lengths,
        hot_table,
        fetched,
        w_in,
        w_out,
        out_grad,
        source.reshape(-1, 1),
        place.reshape(1, -1),
    )
    got = lax.ppermute(far, "table", shift(CORE_GROUPS, 1))
    slot_chunks, hot_chunks = core_sums(near, got)
    pieces = exchange(slot_chunks, "table", Y_GROUPS)
    hot_part = add_up(exchange(hot_chunks, "dp", X_GROUPS))
    shard_place = (wanted // 16 % 4 - x_at) % 4 * 128 + wanted // 64 * 16 + wanted % 16
    back = (y_at - lax.iota(jnp.int32, 4)) % 4
    cores = (core_at + lax.iota(jnp.int32, 2)) % 2
    arriving = (back[:, None] * 2 + cores[None, :]).reshape(table_count)
    shard_place = shard_place.reshape(table_count, cap_size)[arriving].reshape(1, slot_count)
    cold_chunks = shard_sums(shard_place, pieces, shard_rows)
    cold_pieces = exchange(cold_chunks, "dp", X_GROUPS)

    def over_z(rows):
        by_z = rows.astype(jnp.bfloat16).reshape(8, -1, model_width)
        by_z = lax.all_to_all(
            by_z, "dp", split_axis=0, concat_axis=0, tiled=True, axis_index_groups=Z_GROUPS
        )
        return jnp.sum(by_z.astype(jnp.float32), axis=0)

    hot_sum = over_z(hot_part)
    cold_sum = over_z(add_up(cold_pieces))
    hot_sum = add_up(exchange([hot_sum] * 4, "table", Y_GROUPS)).reshape(4, 1, 2, model_width)
    other = lax.ppermute(hot_sum, "table", shift(CORE_GROUPS, 1))
    ordered = jnp.where(
        core_at == 0,
        jnp.concatenate([hot_sum, other], axis=1),
        jnp.concatenate([other, hot_sum], axis=1),
    )
    return (layer_out, ordered.reshape(16, model_width), cold_sum)


def solution(mesh):
    placed = (
        P(),
        P("table", None),
        P(),
        P(),
        P(("table", "dp"), None),
        P(("table", "dp")),
        P(("table", "dp")),
        P(("table", "dp"), None),
        P(("table", "dp"), None),
    )
    return jax.shard_map(
        on_device,
        mesh=mesh,
        in_specs=placed,
        out_specs=(P(("table", "dp"), None), P("dp", None), P(("table", "dp"), None)),
        check_vma=False,
    )
```

```python
import jax
import jax.numpy as jnp
from jax import lax
from jax.experimental import pallas as pl
from jax.experimental.pallas import tpu as pltpu
from jax.sharding import PartitionSpec as P

HEAD = 128


EPS = 1e-06
BLOCK = 128
BACK = 2


def sigmoid(values):
    return 0.5 * jnp.tanh(0.5 * values) + 0.5


def mean_of(values):
    return jnp.mean(values, axis=-1, keepdims=True)


def dot_nn(a, b):
    return jnp.dot(a, b, preferred_element_type=jnp.float32)


def dot_nt(a, b):
    return lax.dot_general(a, b, (((1,), (1,)), ((), ())), preferred_element_type=jnp.float32)


def dot_tn(a, b):
    return lax.dot_general(a, b, (((0,), (0,)), ((), ())), preferred_element_type=jnp.float32)


def pick_kernel(wanted_ref, table_ref, rows_ref):
    takers, cap = wanted_ref.shape
    shard_rows, count = table_ref.shape[0], takers * cap
    wide = jnp.concatenate([wanted_ref[...]] * takers, axis=1)
    taker = lax.broadcasted_iota(jnp.int32, (takers, count), 0)
    lane = lax.broadcasted_iota(jnp.int32, (takers, count), 1)
    own = (lane >= taker * cap) & (lane < taker * cap + cap)
    flat = jnp.sum(jnp.where(own, wide, 0), axis=0, keepdims=True)
    pick = (lax.broadcasted_iota(jnp.int32, (shard_rows, count), 0) == flat).astype(jnp.bfloat16)
    rows_ref[...] = dot_tn(pick, table_ref[...]).astype(jnp.bfloat16)


def pick_rows(wanted, table):
    vmem = pl.BlockSpec(memory_space=pltpu.VMEM)
    return pl.pallas_call(
        pick_kernel,
        out_shape=jax.ShapeDtypeStruct((wanted.size, table.shape[1]), jnp.bfloat16),
        in_specs=[vmem] * 2,
        out_specs=vmem,
        compiler_params=pltpu.CompilerParams(vmem_limit_bytes=4 * 1024 * 1024),
        name="pick_rows",
    )(wanted, table)


def layer_kernel(
    lengths_ref,
    source_ref,
    place_ref,
    fetched_hbm,
    hot_hbm,
    w_in_hbm,
    w_out_hbm,
    out_grad_hbm,
    layer_out_hbm,
    near_ref,
    far_ref,
    fetched_ref,
    hot_ref,
    w_in_ref,
    w_out_ref,
    out_grad_ref,
    layer_out_ref,
    rows_ref,
    normed_ref,
    rstd_ref,
    mixed_ref,
    slope_ref,
    weights_ref,
    dscore_ref,
    attended_ref,
    dvalue_ref,
    dkey_ref,
    dpre_ref,
    dnorm_ref,
    sems,
):
    tokens, width = rows_ref.shape
    hot_rows, slot_count = hot_ref.shape[0], fetched_ref.shape[0]
    inner = w_out_ref.shape[0]
    heads = inner // HEAD
    bf16, f32 = jnp.bfloat16, jnp.float32

    hot_copy = pltpu.make_async_copy(hot_hbm, hot_ref, sems.at[0])
    w_in_copy = pltpu.make_async_copy(w_in_hbm, w_in_ref, sems.at[1])
    w_out_copy = pltpu.make_async_copy(w_out_hbm, w_out_ref, sems.at[2])
    out_grad_copy = pltpu.make_async_copy(out_grad_hbm, out_grad_ref, sems.at[3])
    layer_out_copy = pltpu.make_async_copy(layer_out_ref, layer_out_hbm, sems.at[4])
    fetched_copy = pltpu.make_async_copy(fetched_hbm, fetched_ref, sems.at[5])
    for copy in (hot_copy, fetched_copy, w_in_copy, w_out_copy, out_grad_copy):
        copy.start()
    hot_copy.wait()
    fetched_copy.wait()

    for block in range(tokens // 256):
        at = pl.ds(block * 256, 256)
        source = source_ref[at, :]
        hot_pick = (source == lax.broadcasted_iota(jnp.int32, (256, hot_rows), 1)).astype(bf16)
        slot_pick = (
            source == lax.broadcasted_iota(jnp.int32, (256, slot_count), 1) + hot_rows
        ).astype(bf16)
        rows = dot_nn(hot_pick, hot_ref[...]) + dot_nn(slot_pick, fetched_ref[...])
        centered = rows - mean_of(rows)
        rstd = lax.rsqrt(mean_of(centered * centered) + EPS)
        rows_ref[at, :] = rows.astype(bf16)
        normed_ref[at, :] = (centered * rstd).astype(bf16)
        rstd_ref[at, :] = rstd

    w_in_copy.wait()

    for step in range(4 * inner // 256):
        at = pl.ds(step * 256, 256)
        pre = dot_nn(normed_ref[...], w_in_ref[:, at])
        sig = sigmoid(pre)
        act = pre * sig
        mixed_ref[:, at] = act.astype(bf16)
        slope_ref[:, at] = (sig + act * (1.0 - sig)).astype(bf16)

    def columns(part, head):
        return pl.ds(part * inner + head * HEAD, HEAD)

    for block in range(tokens // BLOCK):
        q_at = pl.ds(block * BLOCK, BLOCK)
        first = max(0, block - BACK)
        reach = (block + 1 - first) * BLOCK
        k_at = pl.ds(first * BLOCK, reach)
        position = lax.broadcasted_iota(jnp.int32, (BLOCK, 1), 0) + block * BLOCK
        begin = jnp.zeros((BLOCK, 1), jnp.int32)
        length = jnp.zeros((BLOCK, 1), jnp.int32)
        end = jnp.int32(0)
        for history in range(lengths_ref.shape[1]):
            start = end
            end = start + lengths_ref[0, history]
            inside = position >= start
            begin = jnp.where(inside, start, begin)
            length = jnp.where(inside, end - start, length)
        key_position = lax.broadcasted_iota(jnp.int32, (BLOCK, reach), 1) + first * BLOCK
        allowed = (key_position <= position) & (key_position >= begin)
        share = jnp.where(allowed, 1.0 / length.astype(f32), 0.0)
        for head in range(heads):
            scores = dot_nt(
                mixed_ref[q_at, columns(2, head)], mixed_ref[k_at, columns(3, head)]
            ) * (HEAD ** -0.5)
            sig = sigmoid(scores)
            act = scores * sig
            weights = (act * share).astype(bf16)
            weights_ref[head, q_at, :reach] = weights
            dscore_ref[head, q_at, :reach] = (
                (sig + act * (1.0 - sig)) * (share * (HEAD ** -0.5))
            ).astype(bf16)
            attended_ref[q_at, pl.ds(head * HEAD, HEAD)] = dot_nn(
                weights, mixed_ref[k_at, columns(1, head)]
            )

    w_out_copy.wait()
    out_grad_copy.wait()

    for block in range(tokens // 256):
        at = pl.ds(block * 256, 256)
        attended = attended_ref[at, :]
        centered = attended - mean_of(attended)
        rstd = lax.rsqrt(mean_of(centered * centered) + EPS)
        unit = centered * rstd
        gate = mixed_ref[at, :inner].astype(f32)
        merged = (unit * gate).astype(bf16)
        layer_out_ref[at, :] = (
            dot_nn(merged, w_out_ref[...]) + rows_ref[at, :].astype(f32)
        ).astype(bf16)
        dmerged = dot_nt(out_grad_ref[at, :], w_out_ref[...])
        dpre_ref[at, :inner] = (dmerged * unit * slope_ref[at, :inner].astype(f32)).astype(bf16)
        dunit = dmerged * gate
        attended_ref[at, :] = rstd * (dunit - mean_of(dunit) - unit * mean_of(dunit * unit))

    layer_out_copy.start()

    dvalue_ref[...] = jnp.zeros_like(dvalue_ref)
    dkey_ref[...] = jnp.zeros_like(dkey_ref)
    for block in range(tokens // BLOCK):
        q_at = pl.ds(block * BLOCK, BLOCK)
        first = max(0, block - BACK)
        reach = (block + 1 - first) * BLOCK
        k_at = pl.ds(first * BLOCK, reach)
        for head in range(heads):
            own = pl.ds(head * HEAD, HEAD)
            dattended = attended_ref[q_at, own].astype(bf16)
            dweights = dot_nt(dattended, mixed_ref[k_at, columns(1, head)])
            dscores = (dweights * dscore_ref[head, q_at, :reach].astype(f32)).astype(bf16)
            dquery = dot_nn(dscores, mixed_ref[k_at, columns(3, head)])
            dpre_ref[q_at, columns(2, head)] = (
                dquery * slope_ref[q_at, columns(2, head)].astype(f32)
            ).astype(bf16)
            dvalue_ref[k_at, own] += dot_tn(weights_ref[head, q_at, :reach], dattended)
            dkey_ref[k_at, own] += dot_tn(dscores, mixed_ref[q_at, columns(2, head)])
    values, keys = pl.ds(inner, inner), pl.ds(3 * inner, inner)
    dpre_ref[:, values] = (dvalue_ref[...] * slope_ref[:, values].astype(f32)).astype(bf16)
    dpre_ref[:, keys] = (dkey_ref[...] * slope_ref[:, keys].astype(f32)).astype(bf16)

    for step in range(width // 256):
        at = pl.ds(step * 256, 256)
        dnorm_ref[:, at] = dot_nt(dpre_ref[...], w_in_ref[at, :])

    for block in range(tokens // 64):
        at = pl.ds(block * 64, 64)
        rstd = rstd_ref[at, :]
        unit = normed_ref[at, :].astype(f32)
        dunit = dnorm_ref[at, :]
        grads = rstd * (dunit - mean_of(dunit) - unit * mean_of(dunit * unit))
        normed_ref[at, :] = (grads + out_grad_ref[at, :].astype(f32)).astype(bf16)

    half = near_ref.shape[0]
    for base, ref in ((half, far_ref), (0, near_ref)):
        pick = (
            lax.broadcasted_iota(jnp.int32, (half, tokens), 0) + base == place_ref[...]
        ).astype(bf16)
        for part in range(2):
            at = pl.ds(part * (width // 2), width // 2)
            ref[:, at] = dot_nn(pick, normed_ref[:, at]).astype(bf16)
    layer_out_copy.wait()


def layer(lengths, hot_table, fetched, w_in, w_out, out_grad, source, place):
    tokens, width = out_grad.shape
    inner = w_out.shape[0]
    heads = inner // HEAD
    half = (hot_table.shape[0] + fetched.shape[0]) // 2
    bf16, f32 = jnp.bfloat16, jnp.float32
    vmem = pl.BlockSpec(memory_space=pltpu.VMEM)
    hbm = pl.BlockSpec(memory_space=pl.ANY)
    reach = (BACK + 1) * BLOCK
    return pl.pallas_call(
        layer_kernel,
        out_shape=(
            jax.ShapeDtypeStruct((tokens, width), bf16),
            jax.ShapeDtypeStruct((half, width), bf16),
            jax.ShapeDtypeStruct((half, width), bf16),
        ),
        in_specs=[pl.BlockSpec(memory_space=pltpu.SMEM)] + [vmem] * 2 + [hbm] * 5,
        out_specs=(hbm, vmem, vmem),
        scratch_shapes=[
            pltpu.VMEM(fetched.shape, bf16),
            pltpu.VMEM(hot_table.shape, bf16),
            pltpu.VMEM(w_in.shape, bf16),
            pltpu.VMEM(w_out.shape, bf16),
            pltpu.VMEM((tokens, width), bf16),
            pltpu.VMEM((tokens, width), bf16),
            pltpu.VMEM((tokens, width), bf16),
            pltpu.VMEM((tokens, width), bf16),
            pltpu.VMEM((tokens, 1), f32),
            pltpu.VMEM((tokens, 4 * inner), bf16),
            pltpu.VMEM((tokens, 4 * inner), bf16),
            pltpu.VMEM((heads, tokens, reach), bf16),
            pltpu.VMEM((heads, tokens, reach), bf16),
            pltpu.VMEM((tokens, inner), f32),
            pltpu.VMEM((tokens, inner), f32),
            pltpu.VMEM((tokens, inner), f32),
            pltpu.VMEM((tokens, 4 * inner), bf16),
            pltpu.VMEM((tokens, width), f32),
            pltpu.SemaphoreType.DMA((6,)),
        ],
        compiler_params=pltpu.CompilerParams(vmem_limit_bytes=58 * 1024 * 1024),
        cost_estimate=pl.CostEstimate(flops=8 * 10**9, bytes_accessed=12 * 10**6, transcendentals=0),
        name="layer",
    )(lengths, source, place, fetched, hot_table, w_in, w_out, out_grad)


def core_sums_kernel(near_ref, got_ref, *out_refs):
    slots = near_ref.shape[0] // 5
    hot = near_ref.shape[0] - slots
    for k in range(4):
        piece = pl.ds(k * slots // 4 + hot, slots // 4)
        out_refs[k][: slots // 4, :] = near_ref[piece, :]
        out_refs[k][slots // 4 :, :] = got_ref[piece, :]
    for k in range(4):
        piece = pl.ds(k * hot // 4, hot // 4)
        total = near_ref[piece, :].astype(jnp.float32) + got_ref[piece, :].astype(jnp.float32)
        out_refs[4 + k][...] = total.astype(jnp.bfloat16)


def core_sums(near, got):
    size, width = near.shape[0] // 5, near.shape[1]
    vmem = pl.BlockSpec(memory_space=pltpu.VMEM)
    out = pl.pallas_call(
        core_sums_kernel,
        out_shape=[jax.ShapeDtypeStruct((size // 2, width), jnp.bfloat16)] * 4
        + [jax.ShapeDtypeStruct((size, width), jnp.bfloat16)] * 4,
        in_specs=[vmem] * 2,
        out_specs=[vmem] * 8,
        compiler_params=pltpu.CompilerParams(vmem_limit_bytes=8 * 1024 * 1024),
        name="core_sums",
    )(near, got)
    return out[:4], out[4:]


def shard_sums_kernel(place_ref, own_ref, first_ref, second_ref, third_ref, *out_refs):
    rows = out_refs[0].shape[0]
    slots = jnp.concatenate(
        [own_ref[...], first_ref[...], second_ref[...], third_ref[...]], axis=0
    )
    for k, ref in enumerate(out_refs):
        pick = (
            lax.broadcasted_iota(jnp.int32, (rows, slots.shape[0]), 0) + k * rows == place_ref[...]
        ).astype(jnp.bfloat16)
        ref[...] = dot_nn(pick, slots).astype(jnp.bfloat16)


def shard_sums(place, pieces, shard_rows):
    width = pieces[0].shape[1]
    vmem = pl.BlockSpec(memory_space=pltpu.VMEM)
    return pl.pallas_call(
        shard_sums_kernel,
        out_shape=[jax.ShapeDtypeStruct((shard_rows // 4, width), jnp.bfloat16)] * 4,
        in_specs=[vmem] * 5,
        out_specs=[vmem] * 4,
        compiler_params=pltpu.CompilerParams(vmem_limit_bytes=4 * 1024 * 1024),
        name="shard_sums",
    )(place, *pieces)


def shift(groups, step):
    return [(g[i], g[(i + step) % len(g)]) for g in groups for i in range(len(g))]


CORE_GROUPS = [[2 * y, 2 * y + 1] for y in range(4)]
Y_GROUPS = [[2 * y + core for y in range(4)] for core in range(2)]
X_GROUPS = [[4 * z + x for x in range(4)] for z in range(8)]
Z_GROUPS = [[4 * z + x for z in range(8)] for x in range(4)]


def exchange(chunks, axis, groups):
    return [
        chunk if k == 0 else lax.ppermute(chunk, axis, shift(groups, k))
        for k, chunk in enumerate(chunks)
    ]


def add_up(pieces):
    here, back_1, back_2, back_3 = [piece.astype(jnp.float32) for piece in pieces]
    return (here + back_2) + (back_1 + back_3)


def on_device(
    hot_table, cold_table, w_in, w_out, seq_lengths, event_hot, event_index, cold_requests, out_grad
):
    table_count = lax.axis_size("table")
    cap_size = cold_requests.shape[1]
    slot_count = table_count * cap_size
    shard_rows = cold_table.shape[0]
    model_width = cold_table.shape[1]
    hot_rows = hot_table.shape[0]
    table_at, dp_at = lax.axis_index("table"), lax.axis_index("dp")
    y_at, core_at, x_at, z_at = table_at // 2, table_at % 2, dp_at % 4, dp_at // 4

    wanted = lax.all_to_all(cold_requests, "table", split_axis=0, concat_axis=0, tiled=True)
    fetched = lax.all_to_all(
        pick_rows(wanted, cold_table).reshape(table_count, cap_size, model_width),
        "table",
        split_axis=0,
        concat_axis=0,
        tiled=True,
    ).reshape(slot_count, model_width)
    wanted = wanted.reshape(slot_count)
    is_hot = event_hot == 1

    hot_dp, hot_t = event_index // 16, (event_index % 16) // 2
    z_step = (hot_dp // 4) ^ z_at
    hot_place = (
        (hot_t % 2 - core_at) % 2 * 320
        + (hot_dp % 4 - x_at) % 4 * 64
        + (z_step % 2 * 4 + z_step // 2 % 2 * 2 + z_step // 4) * 8
        + hot_t // 2 * 2
        + event_index % 2
    )
    slot_t = event_index // 16
    slot_place = (
        (slot_t % 2 - core_at) % 2 * 320
        + 256
        + (slot_t // 2 - y_at) % 4 * 16
        + event_index % 16
    )
    source = jnp.where(is_hot, event_index, event_index + hot_rows)
    place = jnp.where(is_hot, hot_place, slot_place)
    layer_out, near, far = layer(
        seq_lengths,
        hot_table,
        fetched,
        w_in,
        w_out,
        out_grad,
        source.reshape(-1, 1),
        place.reshape(1, -1),
    )
    got = lax.ppermute(far, "table", shift(CORE_GROUPS, 1))
    slot_chunks, hot_chunks = core_sums(near, got)
    pieces = exchange(slot_chunks, "table", Y_GROUPS)
    hot_part = add_up(exchange(hot_chunks, "dp", X_GROUPS))
    shard_place = (wanted // 16 % 4 - x_at) % 4 * 128 + wanted // 64 * 16 + wanted % 16
    back = (y_at - lax.iota(jnp.int32, 4)) % 4
    cores = (core_at + lax.iota(jnp.int32, 2)) % 2
    arriving = (back[:, None] * 2 + cores[None, :]).reshape(table_count)
    shard_place = shard_place.reshape(table_count, cap_size)[arriving].reshape(1, slot_count)
    cold_chunks = shard_sums(shard_place, pieces, shard_rows)
    cold_pieces = exchange(cold_chunks, "dp", X_GROUPS)

    for step in (1, 2, 4):
        half = hot_part.shape[0] // 2
        pairs = [(group[i], group[i ^ step]) for group in Z_GROUPS for i in range(8)]
        sent = lax.ppermute(hot_part[half:].astype(jnp.bfloat16), "dp", pairs)
        hot_part = hot_part[:half] + sent.astype(jnp.float32)
    by_z = add_up(cold_pieces).astype(jnp.bfloat16).reshape(8, -1, model_width)
    by_z = lax.all_to_all(
        by_z, "dp", split_axis=0, concat_axis=0, tiled=True, axis_index_groups=Z_GROUPS
    )
    cold_sum = jnp.sum(by_z.astype(jnp.float32), axis=0)
    hot_sum = add_up(exchange([hot_part] * 4, "table", Y_GROUPS)).reshape(4, 1, 2, model_width)
    other = lax.ppermute(hot_sum, "table", shift(CORE_GROUPS, 1))
    ordered = jnp.where(
        core_at == 0,
        jnp.concatenate([hot_sum, other], axis=1),
        jnp.concatenate([other, hot_sum], axis=1),
    )
    return (layer_out, ordered.reshape(16, model_width), cold_sum)


def solution(mesh):
    placed = (
        P(),
        P("table", None),
        P(),
        P(),
        P(("table", "dp"), None),
        P(("table", "dp")),
        P(("table", "dp")),
        P(("table", "dp"), None),
        P(("table", "dp"), None),
    )
    return jax.shard_map(
        on_device,
        mesh=mesh,
        in_specs=placed,
        out_specs=(P(("table", "dp"), None), P("dp", None), P(("table", "dp"), None)),
        check_vma=False,
    )
```

```python
import jax
import jax.numpy as jnp
from jax import lax
from jax.experimental import pallas as pl
from jax.experimental.pallas import tpu as pltpu
from jax.sharding import PartitionSpec as P

HEAD = 128


EPS = 1e-06
BLOCK = 128
BACK = 2


def sigmoid(values):
    return 0.5 * jnp.tanh(0.5 * values) + 0.5


def mean_of(values):
    return jnp.mean(values, axis=-1, keepdims=True)


def dot_nn(a, b):
    return jnp.dot(a, b, preferred_element_type=jnp.float32)


def dot_nt(a, b):
    return lax.dot_general(a, b, (((1,), (1,)), ((), ())), preferred_element_type=jnp.float32)


def dot_tn(a, b):
    return lax.dot_general(a, b, (((0,), (0,)), ((), ())), preferred_element_type=jnp.float32)


def pick_kernel(wanted_ref, table_ref, rows_ref):
    takers, cap = wanted_ref.shape
    shard_rows, count = table_ref.shape[0], takers * cap
    wide = jnp.concatenate([wanted_ref[...]] * takers, axis=1)
    taker = lax.broadcasted_iota(jnp.int32, (takers, count), 0)
    lane = lax.broadcasted_iota(jnp.int32, (takers, count), 1)
    own = (lane >= taker * cap) & (lane < taker * cap + cap)
    flat = jnp.sum(jnp.where(own, wide, 0), axis=0, keepdims=True)
    pick = (lax.broadcasted_iota(jnp.int32, (shard_rows, count), 0) == flat).astype(jnp.bfloat16)
    rows_ref[...] = dot_tn(pick, table_ref[...]).astype(jnp.bfloat16)


def pick_rows(wanted, table):
    vmem = pl.BlockSpec(memory_space=pltpu.VMEM)
    return pl.pallas_call(
        pick_kernel,
        out_shape=jax.ShapeDtypeStruct((wanted.size, table.shape[1]), jnp.bfloat16),
        in_specs=[vmem] * 2,
        out_specs=vmem,
        compiler_params=pltpu.CompilerParams(vmem_limit_bytes=4 * 1024 * 1024),
        name="pick_rows",
    )(wanted, table)


def layer_kernel(
    lengths_ref,
    source_ref,
    place_ref,
    fetched_hbm,
    hot_hbm,
    w_in_hbm,
    w_out_hbm,
    out_grad_hbm,
    layer_out_hbm,
    near_ref,
    far_ref,
    fetched_ref,
    hot_ref,
    w_in_ref,
    w_out_ref,
    out_grad_ref,
    layer_out_ref,
    rows_ref,
    normed_ref,
    rstd_ref,
    mixed_ref,
    slope_ref,
    weights_ref,
    dscore_ref,
    attended_ref,
    dvalue_ref,
    dkey_ref,
    dpre_ref,
    dnorm_ref,
    sems,
):
    tokens, width = rows_ref.shape
    hot_rows, slot_count = hot_ref.shape[0], fetched_ref.shape[0]
    inner = w_out_ref.shape[0]
    heads = inner // HEAD
    bf16, f32 = jnp.bfloat16, jnp.float32

    hot_copy = pltpu.make_async_copy(hot_hbm, hot_ref, sems.at[0])
    w_in_copy = pltpu.make_async_copy(w_in_hbm, w_in_ref, sems.at[1])
    w_out_copy = pltpu.make_async_copy(w_out_hbm, w_out_ref, sems.at[2])
    out_grad_copy = pltpu.make_async_copy(out_grad_hbm, out_grad_ref, sems.at[3])
    layer_out_copy = pltpu.make_async_copy(layer_out_ref, layer_out_hbm, sems.at[4])
    fetched_copy = pltpu.make_async_copy(fetched_hbm, fetched_ref, sems.at[5])
    for copy in (hot_copy, fetched_copy, w_in_copy, w_out_copy, out_grad_copy):
        copy.start()
    hot_copy.wait()
    fetched_copy.wait()

    for block in range(tokens // 256):
        at = pl.ds(block * 256, 256)
        source = source_ref[at, :]
        hot_pick = (source == lax.broadcasted_iota(jnp.int32, (256, hot_rows), 1)).astype(bf16)
        slot_pick = (
            source == lax.broadcasted_iota(jnp.int32, (256, slot_count), 1) + hot_rows
        ).astype(bf16)
        rows = dot_nn(hot_pick, hot_ref[...]) + dot_nn(slot_pick, fetched_ref[...])
        centered = rows - mean_of(rows)
        rstd = lax.rsqrt(mean_of(centered * centered) + EPS)
        rows_ref[at, :] = rows.astype(bf16)
        normed_ref[at, :] = (centered * rstd).astype(bf16)
        rstd_ref[at, :] = rstd

    w_in_copy.wait()

    for step in range(4 * inner // 256):
        at = pl.ds(step * 256, 256)
        pre = dot_nn(normed_ref[...], w_in_ref[:, at])
        sig = sigmoid(pre)
        act = pre * sig
        mixed_ref[:, at] = act.astype(bf16)
        slope_ref[:, at] = (sig + act * (1.0 - sig)).astype(bf16)

    def columns(part, head):
        return pl.ds(part * inner + head * HEAD, HEAD)

    for block in range(tokens // BLOCK):
        q_at = pl.ds(block * BLOCK, BLOCK)
        first = max(0, block - BACK)
        reach = (block + 1 - first) * BLOCK
        k_at = pl.ds(first * BLOCK, reach)
        position = lax.broadcasted_iota(jnp.int32, (BLOCK, 1), 0) + block * BLOCK
        begin = jnp.zeros((BLOCK, 1), jnp.int32)
        length = jnp.zeros((BLOCK, 1), jnp.int32)
        end = jnp.int32(0)
        for history in range(lengths_ref.shape[1]):
            start = end
            end = start + lengths_ref[0, history]
            inside = position >= start
            begin = jnp.where(inside, start, begin)
            length = jnp.where(inside, end - start, length)
        key_position = lax.broadcasted_iota(jnp.int32, (BLOCK, reach), 1) + first * BLOCK
        allowed = (key_position <= position) & (key_position >= begin)
        share = jnp.where(allowed, 1.0 / length.astype(f32), 0.0)
        for head in range(heads):
            scores = dot_nt(
                mixed_ref[q_at, columns(2, head)], mixed_ref[k_at, columns(3, head)]
            ) * (HEAD ** -0.5)
            sig = sigmoid(scores)
            act = scores * sig
            weights = (act * share).astype(bf16)
            weights_ref[head, q_at, :reach] = weights
            dscore_ref[head, q_at, :reach] = (
                (sig + act * (1.0 - sig)) * (share * (HEAD ** -0.5))
            ).astype(bf16)
            attended_ref[q_at, pl.ds(head * HEAD, HEAD)] = dot_nn(
                weights, mixed_ref[k_at, columns(1, head)]
            )

    w_out_copy.wait()
    out_grad_copy.wait()

    for block in range(tokens // 256):
        at = pl.ds(block * 256, 256)
        attended = attended_ref[at, :]
        centered = attended - mean_of(attended)
        rstd = lax.rsqrt(mean_of(centered * centered) + EPS)
        unit = centered * rstd
        gate = mixed_ref[at, :inner].astype(f32)
        merged = (unit * gate).astype(bf16)
        layer_out_ref[at, :] = (
            dot_nn(merged, w_out_ref[...]) + rows_ref[at, :].astype(f32)
        ).astype(bf16)
        dmerged = dot_nt(out_grad_ref[at, :], w_out_ref[...])
        dpre_ref[at, :inner] = (dmerged * unit * slope_ref[at, :inner].astype(f32)).astype(bf16)
        dunit = dmerged * gate
        attended_ref[at, :] = rstd * (dunit - mean_of(dunit) - unit * mean_of(dunit * unit))

    layer_out_copy.start()

    dvalue_ref[...] = jnp.zeros_like(dvalue_ref)
    dkey_ref[...] = jnp.zeros_like(dkey_ref)
    for block in range(tokens // BLOCK):
        q_at = pl.ds(block * BLOCK, BLOCK)
        first = max(0, block - BACK)
        reach = (block + 1 - first) * BLOCK
        k_at = pl.ds(first * BLOCK, reach)
        for head in range(heads):
            own = pl.ds(head * HEAD, HEAD)
            dattended = attended_ref[q_at, own].astype(bf16)
            dweights = dot_nt(dattended, mixed_ref[k_at, columns(1, head)])
            dscores = (dweights * dscore_ref[head, q_at, :reach].astype(f32)).astype(bf16)
            dquery = dot_nn(dscores, mixed_ref[k_at, columns(3, head)])
            dpre_ref[q_at, columns(2, head)] = (
                dquery * slope_ref[q_at, columns(2, head)].astype(f32)
            ).astype(bf16)
            dvalue_ref[k_at, own] += dot_tn(weights_ref[head, q_at, :reach], dattended)
            dkey_ref[k_at, own] += dot_tn(dscores, mixed_ref[q_at, columns(2, head)])
    values, keys = pl.ds(inner, inner), pl.ds(3 * inner, inner)
    dpre_ref[:, values] = (dvalue_ref[...] * slope_ref[:, values].astype(f32)).astype(bf16)
    dpre_ref[:, keys] = (dkey_ref[...] * slope_ref[:, keys].astype(f32)).astype(bf16)

    for step in range(width // 256):
        at = pl.ds(step * 256, 256)
        dnorm_ref[:, at] = dot_nt(dpre_ref[...], w_in_ref[at, :])

    for block in range(tokens // 64):
        at = pl.ds(block * 64, 64)
        rstd = rstd_ref[at, :]
        unit = normed_ref[at, :].astype(f32)
        dunit = dnorm_ref[at, :]
        grads = rstd * (dunit - mean_of(dunit) - unit * mean_of(dunit * unit))
        normed_ref[at, :] = (grads + out_grad_ref[at, :].astype(f32)).astype(bf16)

    half = near_ref.shape[0]
    for base, ref in ((half, far_ref), (0, near_ref)):
        pick = (
            lax.broadcasted_iota(jnp.int32, (half, tokens), 0) + base == place_ref[...]
        ).astype(bf16)
        for part in range(2):
            at = pl.ds(part * (width // 2), width // 2)
            ref[:, at] = dot_nn(pick, normed_ref[:, at]).astype(bf16)
    layer_out_copy.wait()


def layer(lengths, hot_table, fetched, w_in, w_out, out_grad, source, place):
    tokens, width = out_grad.shape
    inner = w_out.shape[0]
    heads = inner // HEAD
    half = (hot_table.shape[0] + fetched.shape[0]) // 2
    bf16, f32 = jnp.bfloat16, jnp.float32
    vmem = pl.BlockSpec(memory_space=pltpu.VMEM)
    hbm = pl.BlockSpec(memory_space=pl.ANY)
    reach = (BACK + 1) * BLOCK
    return pl.pallas_call(
        layer_kernel,
        out_shape=(
            jax.ShapeDtypeStruct((tokens, width), bf16),
            jax.ShapeDtypeStruct((half, width), bf16),
            jax.ShapeDtypeStruct((half, width), bf16),
        ),
        in_specs=[pl.BlockSpec(memory_space=pltpu.SMEM)] + [vmem] * 2 + [hbm] * 5,
        out_specs=(hbm, vmem, vmem),
        scratch_shapes=[
            pltpu.VMEM(fetched.shape, bf16),
            pltpu.VMEM(hot_table.shape, bf16),
            pltpu.VMEM(w_in.shape, bf16),
            pltpu.VMEM(w_out.shape, bf16),
            pltpu.VMEM((tokens, width), bf16),
            pltpu.VMEM((tokens, width), bf16),
            pltpu.VMEM((tokens, width), bf16),
            pltpu.VMEM((tokens, width), bf16),
            pltpu.VMEM((tokens, 1), f32),
            pltpu.VMEM((tokens, 4 * inner), bf16),
            pltpu.VMEM((tokens, 4 * inner), bf16),
            pltpu.VMEM((heads, tokens, reach), bf16),
            pltpu.VMEM((heads, tokens, reach), bf16),
            pltpu.VMEM((tokens, inner), f32),
            pltpu.VMEM((tokens, inner), f32),
            pltpu.VMEM((tokens, inner), f32),
            pltpu.VMEM((tokens, 4 * inner), bf16),
            pltpu.VMEM((tokens, width), f32),
            pltpu.SemaphoreType.DMA((6,)),
        ],
        compiler_params=pltpu.CompilerParams(vmem_limit_bytes=52 * 1024 * 1024),
        cost_estimate=pl.CostEstimate(flops=8 * 10**9, bytes_accessed=12 * 10**6, transcendentals=0),
        name="layer",
    )(lengths, source, place, fetched, hot_table, w_in, w_out, out_grad)


def core_sums_kernel(near_ref, got_ref, *out_refs):
    slots = near_ref.shape[0] // 5
    hot = near_ref.shape[0] - slots
    for k in range(4):
        piece = pl.ds(k * slots // 4 + hot, slots // 4)
        out_refs[k][: slots // 4, :] = near_ref[piece, :]
        out_refs[k][slots // 4 :, :] = got_ref[piece, :]
    for k in range(4):
        piece = pl.ds(k * hot // 4, hot // 4)
        total = near_ref[piece, :].astype(jnp.float32) + got_ref[piece, :].astype(jnp.float32)
        out_refs[4 + k][...] = total.astype(jnp.bfloat16)


def core_sums(near, got):
    size, width = near.shape[0] // 5, near.shape[1]
    vmem = pl.BlockSpec(memory_space=pltpu.VMEM)
    out = pl.pallas_call(
        core_sums_kernel,
        out_shape=[jax.ShapeDtypeStruct((size // 2, width), jnp.bfloat16)] * 4
        + [jax.ShapeDtypeStruct((size, width), jnp.bfloat16)] * 4,
        in_specs=[vmem] * 2,
        out_specs=[vmem] * 8,
        compiler_params=pltpu.CompilerParams(vmem_limit_bytes=8 * 1024 * 1024),
        name="core_sums",
    )(near, got)
    return out[:4], out[4:]


def shard_sums_kernel(place_ref, own_ref, first_ref, second_ref, third_ref, *out_refs):
    rows = out_refs[0].shape[0]
    slots = jnp.concatenate(
        [own_ref[...], first_ref[...], second_ref[...], third_ref[...]], axis=0
    )
    for k, ref in enumerate(out_refs):
        pick = (
            lax.broadcasted_iota(jnp.int32, (rows, slots.shape[0]), 0) + k * rows == place_ref[...]
        ).astype(jnp.bfloat16)
        ref[...] = dot_nn(pick, slots).astype(jnp.bfloat16)


def shard_sums(place, pieces, shard_rows):
    width = pieces[0].shape[1]
    vmem = pl.BlockSpec(memory_space=pltpu.VMEM)
    return pl.pallas_call(
        shard_sums_kernel,
        out_shape=[jax.ShapeDtypeStruct((shard_rows // 4, width), jnp.bfloat16)] * 4,
        in_specs=[vmem] * 5,
        out_specs=[vmem] * 4,
        compiler_params=pltpu.CompilerParams(vmem_limit_bytes=4 * 1024 * 1024),
        name="shard_sums",
    )(place, *pieces)


def shift(groups, step):
    return [(g[i], g[(i + step) % len(g)]) for g in groups for i in range(len(g))]


CORE_GROUPS = [[2 * y, 2 * y + 1] for y in range(4)]
Y_GROUPS = [[2 * y + core for y in range(4)] for core in range(2)]
X_GROUPS = [[4 * z + x for x in range(4)] for z in range(8)]
Z_GROUPS = [[4 * z + x for z in range(8)] for x in range(4)]


def exchange(chunks, axis, groups):
    return [
        chunk if k == 0 else lax.ppermute(chunk, axis, shift(groups, k))
        for k, chunk in enumerate(chunks)
    ]


def add_up(pieces):
    here, back_1, back_2, back_3 = [piece.astype(jnp.float32) for piece in pieces]
    return (here + back_2) + (back_1 + back_3)


def on_device(
    hot_table, cold_table, w_in, w_out, seq_lengths, event_hot, event_index, cold_requests, out_grad
):
    table_count = lax.axis_size("table")
    cap_size = cold_requests.shape[1]
    slot_count = table_count * cap_size
    shard_rows = cold_table.shape[0]
    model_width = cold_table.shape[1]
    hot_rows = hot_table.shape[0]
    table_at, dp_at = lax.axis_index("table"), lax.axis_index("dp")
    y_at, core_at, x_at, z_at = table_at // 2, table_at % 2, dp_at % 4, dp_at // 4

    wanted = lax.all_to_all(cold_requests, "table", split_axis=0, concat_axis=0, tiled=True)
    fetched = lax.all_to_all(
        pick_rows(wanted, cold_table).reshape(table_count, cap_size, model_width),
        "table",
        split_axis=0,
        concat_axis=0,
        tiled=True,
    ).reshape(slot_count, model_width)
    wanted = wanted.reshape(slot_count)
    is_hot = event_hot == 1

    hot_dp, hot_t = event_index // 16, (event_index % 16) // 2
    z_step = (hot_dp // 4) ^ z_at
    hot_place = (
        (hot_t % 2 - core_at) % 2 * 320
        + (hot_dp % 4 - x_at) % 4 * 64
        + (z_step % 2 * 4 + z_step // 2 % 2 * 2 + z_step // 4) * 8
        + hot_t // 2 * 2
        + event_index % 2
    )
    slot_t = event_index // 16
    slot_place = (
        (slot_t % 2 - core_at) % 2 * 320
        + 256
        + (slot_t // 2 - y_at) % 4 * 16
        + event_index % 16
    )
    source = jnp.where(is_hot, event_index, event_index + hot_rows)
    place = jnp.where(is_hot, hot_place, slot_place)
    layer_out, near, far = layer(
        seq_lengths,
        hot_table,
        fetched,
        w_in,
        w_out,
        out_grad,
        source.reshape(-1, 1),
        place.reshape(1, -1),
    )
    got = lax.ppermute(far, "table", shift(CORE_GROUPS, 1))
    slot_chunks, hot_chunks = core_sums(near, got)
    pieces = exchange(slot_chunks, "table", Y_GROUPS)
    hot_part = add_up(exchange(hot_chunks, "dp", X_GROUPS))
    shard_place = (wanted // 16 % 4 - x_at) % 4 * 128 + wanted // 64 * 16 + wanted % 16
    back = (y_at - lax.iota(jnp.int32, 4)) % 4
    cores = (core_at + lax.iota(jnp.int32, 2)) % 2
    arriving = (back[:, None] * 2 + cores[None, :]).reshape(table_count)
    shard_place = shard_place.reshape(table_count, cap_size)[arriving].reshape(1, slot_count)
    cold_chunks = shard_sums(shard_place, pieces, shard_rows)
    cold_pieces = exchange(cold_chunks, "dp", X_GROUPS)

    for step in (1, 2, 4):
        half = hot_part.shape[0] // 2
        pairs = [(group[i], group[i ^ step]) for group in Z_GROUPS for i in range(8)]
        sent = lax.ppermute(hot_part[half:].astype(jnp.bfloat16), "dp", pairs)
        hot_part = hot_part[:half] + sent.astype(jnp.float32)
    by_z = add_up(cold_pieces).astype(jnp.bfloat16).reshape(8, -1, model_width)
    by_z = lax.all_to_all(
        by_z, "dp", split_axis=0, concat_axis=0, tiled=True, axis_index_groups=Z_GROUPS
    )
    cold_sum = jnp.sum(by_z.astype(jnp.float32), axis=0)
    hot_sum = add_up(exchange([hot_part] * 4, "table", Y_GROUPS)).reshape(4, 1, 2, model_width)
    other = lax.ppermute(hot_sum, "table", shift(CORE_GROUPS, 1))
    ordered = jnp.where(
        core_at == 0,
        jnp.concatenate([hot_sum, other], axis=1),
        jnp.concatenate([other, hot_sum], axis=1),
    )
    return (layer_out, ordered.reshape(16, model_width), cold_sum)


def solution(mesh):
    placed = (
        P(),
        P("table", None),
        P(),
        P(),
        P(("table", "dp"), None),
        P(("table", "dp")),
        P(("table", "dp")),
        P(("table", "dp"), None),
        P(("table", "dp"), None),
    )
    return jax.shard_map(
        on_device,
        mesh=mesh,
        in_specs=placed,
        out_specs=(P(("table", "dp"), None), P("dp", None), P(("table", "dp"), None)),
        check_vma=False,
    )
```

```python
import jax
import jax.numpy as jnp
from jax import lax
from jax.experimental import pallas as pl
from jax.experimental.pallas import tpu as pltpu
from jax.sharding import PartitionSpec as P

HEAD = 128


EPS = 1e-06
BLOCK = 128
BACK = 2


def sigmoid(values):
    return 0.5 * jnp.tanh(0.5 * values) + 0.5


def mean_of(values):
    return jnp.mean(values, axis=-1, keepdims=True)


def dot_nn(a, b):
    return jnp.dot(a, b, preferred_element_type=jnp.float32)


def dot_nt(a, b):
    return lax.dot_general(a, b, (((1,), (1,)), ((), ())), preferred_element_type=jnp.float32)


def dot_tn(a, b):
    return lax.dot_general(a, b, (((0,), (0,)), ((), ())), preferred_element_type=jnp.float32)


def bring_kernel(after_ref, table_hbm, table_ref, sem):
    copy = pltpu.make_async_copy(table_hbm, table_ref, sem)
    copy.start()
    copy.wait()


def bring(table, after):
    vmem = pl.BlockSpec(memory_space=pltpu.VMEM)
    return pl.pallas_call(
        bring_kernel,
        out_shape=jax.ShapeDtypeStruct(table.shape, table.dtype),
        in_specs=[vmem, pl.BlockSpec(memory_space=pl.ANY)],
        out_specs=vmem,
        scratch_shapes=[pltpu.SemaphoreType.DMA],
        compiler_params=pltpu.CompilerParams(vmem_limit_bytes=4 * 1024 * 1024),
        cost_estimate=pl.CostEstimate(flops=0, bytes_accessed=2 * 10**6, transcendentals=0),
        name="bring",
    )(after, table)


def pick_kernel(wanted_ref, table_ref, rows_ref):
    takers, cap = wanted_ref.shape
    shard_rows, count = table_ref.shape[0], takers * cap
    wide = jnp.concatenate([wanted_ref[...]] * takers, axis=1)
    taker = lax.broadcasted_iota(jnp.int32, (takers, count), 0)
    lane = lax.broadcasted_iota(jnp.int32, (takers, count), 1)
    own = (lane >= taker * cap) & (lane < taker * cap + cap)
    flat = jnp.sum(jnp.where(own, wide, 0), axis=0, keepdims=True)
    pick = (lax.broadcasted_iota(jnp.int32, (shard_rows, count), 0) == flat).astype(jnp.bfloat16)
    rows_ref[...] = dot_tn(pick, table_ref[...]).astype(jnp.bfloat16)


def pick_rows(wanted, table):
    vmem = pl.BlockSpec(memory_space=pltpu.VMEM)
    return pl.pallas_call(
        pick_kernel,
        out_shape=jax.ShapeDtypeStruct((wanted.size, table.shape[1]), jnp.bfloat16),
        in_specs=[vmem] * 2,
        out_specs=vmem,
        compiler_params=pltpu.CompilerParams(vmem_limit_bytes=4 * 1024 * 1024),
        name="pick_rows",
    )(wanted, table)


def layer_kernel(
    ends_ref,
    source_ref,
    place_ref,
    fetched_hbm,
    hot_hbm,
    w_in_hbm,
    w_out_hbm,
    out_grad_hbm,
    layer_out_hbm,
    near_ref,
    far_ref,
    fetched_ref,
    hot_ref,
    w_in_ref,
    w_out_ref,
    out_grad_ref,
    layer_out_ref,
    rows_ref,
    normed_ref,
    rstd_ref,
    mixed_ref,
    slope_ref,
    weights_ref,
    dscore_ref,
    attended_ref,
    dvalue_ref,
    dkey_ref,
    dpre_ref,
    dnorm_ref,
    sems,
):
    tokens, width = rows_ref.shape
    hot_rows, slot_count = hot_ref.shape[0], fetched_ref.shape[0]
    inner = w_out_ref.shape[0]
    heads = inner // HEAD
    bf16, f32 = jnp.bfloat16, jnp.float32

    hot_copy = pltpu.make_async_copy(hot_hbm, hot_ref, sems.at[0])
    w_in_copy = pltpu.make_async_copy(w_in_hbm, w_in_ref, sems.at[1])
    w_out_copy = pltpu.make_async_copy(w_out_hbm, w_out_ref, sems.at[2])
    out_grad_copy = pltpu.make_async_copy(out_grad_hbm, out_grad_ref, sems.at[3])
    layer_out_copy = pltpu.make_async_copy(layer_out_ref, layer_out_hbm, sems.at[4])
    fetched_copy = pltpu.make_async_copy(fetched_hbm, fetched_ref, sems.at[5])
    for copy in (hot_copy, fetched_copy, w_in_copy, w_out_copy, out_grad_copy):
        copy.start()
    hot_copy.wait()

    for block in range(tokens // 256):
        at = pl.ds(block * 256, 256)
        source = source_ref[at, :]
        hot_pick = (source == lax.broadcasted_iota(jnp.int32, (256, hot_rows), 1)).astype(bf16)
        slot_pick = (
            source == lax.broadcasted_iota(jnp.int32, (256, slot_count), 1) + hot_rows
        ).astype(bf16)
        rows = dot_nn(hot_pick, hot_ref[...])
        if block == 0:
            fetched_copy.wait()
        rows = rows + dot_nn(slot_pick, fetched_ref[...])
        centered = rows - mean_of(rows)
        rstd = lax.rsqrt(mean_of(centered * centered) + EPS)
        rows_ref[at, :] = rows.astype(bf16)
        normed_ref[at, :] = (centered * rstd).astype(bf16)
        rstd_ref[at, :] = rstd

    w_in_copy.wait()

    for step in range(4 * inner // 256):
        at = pl.ds(step * 256, 256)
        pre = dot_nn(normed_ref[...], w_in_ref[:, at])
        sig = sigmoid(pre)
        act = pre * sig
        mixed_ref[:, at] = act.astype(bf16)
        slope_ref[:, at] = (sig + act * (1.0 - sig)).astype(bf16)

    def columns(part, head):
        return pl.ds(part * inner + head * HEAD, HEAD)

    for block in range(tokens // BLOCK):
        q_at = pl.ds(block * BLOCK, BLOCK)
        first = max(0, block - BACK)
        reach = (block + 1 - first) * BLOCK
        k_at = pl.ds(first * BLOCK, reach)
        position = lax.broadcasted_iota(jnp.int32, (BLOCK, 1), 0) + block * BLOCK
        begin = jnp.zeros((BLOCK, 1), jnp.int32)
        length = jnp.zeros((BLOCK, 1), jnp.int32)
        end = jnp.int32(0)
        for history in range(ends_ref.shape[1]):
            start = end
            end = ends_ref[0, history]
            inside = position >= start
            begin = jnp.where(inside, start, begin)
            length = jnp.where(inside, end - start, length)
        key_position = lax.broadcasted_iota(jnp.int32, (BLOCK, reach), 1) + first * BLOCK
        allowed = (key_position <= position) & (key_position >= begin)
        share = jnp.where(allowed, 1.0 / length.astype(f32), 0.0)
        for head in range(heads):
            scores = dot_nt(
                mixed_ref[q_at, columns(2, head)], mixed_ref[k_at, columns(3, head)]
            ) * (HEAD ** -0.5)
            sig = sigmoid(scores)
            act = scores * sig
            weights = (act * share).astype(bf16)
            weights_ref[head, q_at, :reach] = weights
            dscore_ref[head, q_at, :reach] = (
                (sig + act * (1.0 - sig)) * (share * (HEAD ** -0.5))
            ).astype(bf16)
            attended_ref[q_at, pl.ds(head * HEAD, HEAD)] = dot_nn(
                weights, mixed_ref[k_at, columns(1, head)]
            )

    w_out_copy.wait()
    out_grad_copy.wait()

    for block in range(tokens // 256):
        at = pl.ds(block * 256, 256)
        attended = attended_ref[at, :]
        centered = attended - mean_of(attended)
        rstd = lax.rsqrt(mean_of(centered * centered) + EPS)
        unit = centered * rstd
        gate = mixed_ref[at, :inner].astype(f32)
        merged = (unit * gate).astype(bf16)
        layer_out_ref[at, :] = (
            dot_nn(merged, w_out_ref[...]) + rows_ref[at, :].astype(f32)
        ).astype(bf16)
        dmerged = dot_nt(out_grad_ref[at, :], w_out_ref[...])
        dpre_ref[at, :inner] = (dmerged * unit * slope_ref[at, :inner].astype(f32)).astype(bf16)
        dunit = dmerged * gate
        attended_ref[at, :] = rstd * (dunit - mean_of(dunit) - unit * mean_of(dunit * unit))

    layer_out_copy.start()

    dvalue_ref[...] = jnp.zeros_like(dvalue_ref)
    dkey_ref[...] = jnp.zeros_like(dkey_ref)
    for block in range(tokens // BLOCK):
        q_at = pl.ds(block * BLOCK, BLOCK)
        first = max(0, block - BACK)
        reach = (block + 1 - first) * BLOCK
        k_at = pl.ds(first * BLOCK, reach)
        for head in range(heads):
            own = pl.ds(head * HEAD, HEAD)
            dattended = attended_ref[q_at, own].astype(bf16)
            dweights = dot_nt(dattended, mixed_ref[k_at, columns(1, head)])
            dscores = (dweights * dscore_ref[head, q_at, :reach].astype(f32)).astype(bf16)
            dquery = dot_nn(dscores, mixed_ref[k_at, columns(3, head)])
            dpre_ref[q_at, columns(2, head)] = (
                dquery * slope_ref[q_at, columns(2, head)].astype(f32)
            ).astype(bf16)
            dvalue_ref[k_at, own] += dot_tn(weights_ref[head, q_at, :reach], dattended)
            dkey_ref[k_at, own] += dot_tn(dscores, mixed_ref[q_at, columns(2, head)])
    values, keys = pl.ds(inner, inner), pl.ds(3 * inner, inner)
    dpre_ref[:, values] = (dvalue_ref[...] * slope_ref[:, values].astype(f32)).astype(bf16)
    dpre_ref[:, keys] = (dkey_ref[...] * slope_ref[:, keys].astype(f32)).astype(bf16)

    for step in range(width // 256):
        at = pl.ds(step * 256, 256)
        dnorm_ref[:, at] = dot_nt(dpre_ref[...], w_in_ref[at, :])

    for block in range(tokens // 64):
        at = pl.ds(block * 64, 64)
        rstd = rstd_ref[at, :]
        unit = normed_ref[at, :].astype(f32)
        dunit = dnorm_ref[at, :]
        grads = rstd * (dunit - mean_of(dunit) - unit * mean_of(dunit * unit))
        normed_ref[at, :] = (grads + out_grad_ref[at, :].astype(f32)).astype(bf16)

    half = near_ref.shape[0]
    for base, ref in ((half, far_ref), (0, near_ref)):
        pick = (
            lax.broadcasted_iota(jnp.int32, (half, tokens), 0) + base == place_ref[...]
        ).astype(bf16)
        for part in range(2):
            at = pl.ds(part * (width // 2), width // 2)
            ref[:, at] = dot_nn(pick, normed_ref[:, at]).astype(bf16)
    layer_out_copy.wait()


def layer(lengths, hot_table, fetched, w_in, w_out, out_grad, source, place):
    tokens, width = out_grad.shape
    inner = w_out.shape[0]
    heads = inner // HEAD
    half = (hot_table.shape[0] + fetched.shape[0]) // 2
    bf16, f32 = jnp.bfloat16, jnp.float32
    vmem = pl.BlockSpec(memory_space=pltpu.VMEM)
    hbm = pl.BlockSpec(memory_space=pl.ANY)
    reach = (BACK + 1) * BLOCK
    before = lax.iota(jnp.int32, lengths.shape[1])
    ends = jnp.sum(
        jnp.where(before[:, None] <= before[None, :], lengths.reshape(-1, 1), 0),
        axis=0,
        keepdims=True,
    )
    return pl.pallas_call(
        layer_kernel,
        out_shape=(
            jax.ShapeDtypeStruct((tokens, width), bf16),
            jax.ShapeDtypeStruct((half, width), bf16),
            jax.ShapeDtypeStruct((half, width), bf16),
        ),
        in_specs=[pl.BlockSpec(memory_space=pltpu.SMEM)] + [vmem] * 2 + [hbm] * 5,
        out_specs=(hbm, vmem, vmem),
        scratch_shapes=[
            pltpu.VMEM(fetched.shape, bf16),
            pltpu.VMEM(hot_table.shape, bf16),
            pltpu.VMEM(w_in.shape, bf16),
            pltpu.VMEM(w_out.shape, bf16),
            pltpu.VMEM((tokens, width), bf16),
            pltpu.VMEM((tokens, width), bf16),
            pltpu.VMEM((tokens, width), bf16),
            pltpu.VMEM((tokens, width), bf16),
            pltpu.VMEM((tokens, 1), f32),
            pltpu.VMEM((tokens, 4 * inner), bf16),
            pltpu.VMEM((tokens, 4 * inner), bf16),
            pltpu.VMEM((heads, tokens, reach), bf16),
            pltpu.VMEM((heads, tokens, reach), bf16),
            pltpu.VMEM((tokens, inner), f32),
            pltpu.VMEM((tokens, inner), f32),
            pltpu.VMEM((tokens, inner), f32),
            pltpu.VMEM((tokens, 4 * inner), bf16),
            pltpu.VMEM((tokens, width), f32),
            pltpu.SemaphoreType.DMA((6,)),
        ],
        compiler_params=pltpu.CompilerParams(vmem_limit_bytes=52 * 1024 * 1024),
        cost_estimate=pl.CostEstimate(flops=8 * 10**9, bytes_accessed=12 * 10**6, transcendentals=0),
        name="layer",
    )(ends, source, place, fetched, hot_table, w_in, w_out, out_grad)


def core_sums_kernel(near_ref, got_ref, *out_refs):
    slots = near_ref.shape[0] // 5
    hot = near_ref.shape[0] - slots
    for k in range(4):
        piece = pl.ds(k * slots // 4 + hot, slots // 4)
        out_refs[k][: slots // 4, :] = near_ref[piece, :]
        out_refs[k][slots // 4 :, :] = got_ref[piece, :]
    for k in range(4):
        piece = pl.ds(k * hot // 4, hot // 4)
        total = near_ref[piece, :].astype(jnp.float32) + got_ref[piece, :].astype(jnp.float32)
        out_refs[4 + k][...] = total.astype(jnp.bfloat16)


def core_sums(near, got):
    size, width = near.shape[0] // 5, near.shape[1]
    vmem = pl.BlockSpec(memory_space=pltpu.VMEM)
    out = pl.pallas_call(
        core_sums_kernel,
        out_shape=[jax.ShapeDtypeStruct((size // 2, width), jnp.bfloat16)] * 4
        + [jax.ShapeDtypeStruct((size, width), jnp.bfloat16)] * 4,
        in_specs=[vmem] * 2,
        out_specs=[vmem] * 8,
        compiler_params=pltpu.CompilerParams(vmem_limit_bytes=8 * 1024 * 1024),
        name="core_sums",
    )(near, got)
    return out[:4], out[4:]


def shard_sums_kernel(place_ref, own_ref, first_ref, second_ref, third_ref, *out_refs):
    rows = out_refs[0].shape[0]
    slots = jnp.concatenate(
        [own_ref[...], first_ref[...], second_ref[...], third_ref[...]], axis=0
    )
    for k, ref in enumerate(out_refs):
        pick = (
            lax.broadcasted_iota(jnp.int32, (rows, slots.shape[0]), 0) + k * rows == place_ref[...]
        ).astype(jnp.bfloat16)
        ref[...] = dot_nn(pick, slots).astype(jnp.bfloat16)


def shard_sums(place, pieces, shard_rows):
    width = pieces[0].shape[1]
    vmem = pl.BlockSpec(memory_space=pltpu.VMEM)
    return pl.pallas_call(
        shard_sums_kernel,
        out_shape=[jax.ShapeDtypeStruct((shard_rows // 4, width), jnp.bfloat16)] * 4,
        in_specs=[vmem] * 5,
        out_specs=[vmem] * 4,
        compiler_params=pltpu.CompilerParams(vmem_limit_bytes=4 * 1024 * 1024),
        name="shard_sums",
    )(place, *pieces)


def shift(groups, step):
    return [(g[i], g[(i + step) % len(g)]) for g in groups for i in range(len(g))]


CORE_GROUPS = [[2 * y, 2 * y + 1] for y in range(4)]
Y_GROUPS = [[2 * y + core for y in range(4)] for core in range(2)]
X_GROUPS = [[4 * z + x for x in range(4)] for z in range(8)]
Z_GROUPS = [[4 * z + x for z in range(8)] for x in range(4)]


def exchange(chunks, axis, groups):
    return [
        chunk if k == 0 else lax.ppermute(chunk, axis, shift(groups, k))
        for k, chunk in enumerate(chunks)
    ]


def add_up(pieces):
    here, back_1, back_2, back_3 = [piece.astype(jnp.float32) for piece in pieces]
    return (here + back_2) + (back_1 + back_3)


def on_device(
    hot_table, cold_table, w_in, w_out, seq_lengths, event_hot, event_index, cold_requests, out_grad
):
    table_count = lax.axis_size("table")
    cap_size = cold_requests.shape[1]
    slot_count = table_count * cap_size
    shard_rows = cold_table.shape[0]
    model_width = cold_table.shape[1]
    hot_rows = hot_table.shape[0]
    table_at, dp_at = lax.axis_index("table"), lax.axis_index("dp")
    y_at, core_at, x_at, z_at = table_at // 2, table_at % 2, dp_at % 4, dp_at // 4

    wanted = lax.all_to_all(cold_requests, "table", split_axis=0, concat_axis=0, tiled=True)
    fetched = lax.all_to_all(
        pick_rows(wanted, bring(cold_table, cold_requests)).reshape(table_count, cap_size, model_width),
        "table",
        split_axis=0,
        concat_axis=0,
        tiled=True,
    ).reshape(slot_count, model_width)
    wanted = wanted.reshape(slot_count)
    is_hot = event_hot == 1

    hot_dp, hot_t = event_index // 16, (event_index % 16) // 2
    z_step = (hot_dp // 4) ^ z_at
    hot_place = (
        (hot_t % 2 - core_at) % 2 * 320
        + (hot_dp % 4 - x_at) % 4 * 64
        + (z_step % 2 * 4 + z_step // 2 % 2 * 2 + z_step // 4) * 8
        + hot_t // 2 * 2
        + event_index % 2
    )
    slot_t = event_index // 16
    slot_place = (
        (slot_t % 2 - core_at) % 2 * 320
        + 256
        + (slot_t // 2 - y_at) % 4 * 16
        + event_index % 16
    )
    source = jnp.where(is_hot, event_index, event_index + hot_rows)
    place = jnp.where(is_hot, hot_place, slot_place)
    layer_out, near, far = layer(
        seq_lengths,
        hot_table,
        fetched,
        w_in,
        w_out,
        out_grad,
        source.reshape(-1, 1),
        place.reshape(1, -1),
    )
    got = lax.ppermute(far, "table", shift(CORE_GROUPS, 1))
    slot_chunks, hot_chunks = core_sums(near, got)
    pieces = exchange(slot_chunks, "table", Y_GROUPS)
    hot_part = add_up(exchange(hot_chunks, "dp", X_GROUPS))
    shard_place = (wanted // 16 % 4 - x_at) % 4 * 128 + wanted // 64 * 16 + wanted % 16
    back = (y_at - lax.iota(jnp.int32, 4)) % 4
    cores = (core_at + lax.iota(jnp.int32, 2)) % 2
    arriving = (back[:, None] * 2 + cores[None, :]).reshape(table_count)
    shard_place = shard_place.reshape(table_count, cap_size)[arriving].reshape(1, slot_count)
    cold_chunks = shard_sums(shard_place, pieces, shard_rows)
    cold_pieces = exchange(cold_chunks, "dp", X_GROUPS)

    for step in (1, 2, 4):
        half = hot_part.shape[0] // 2
        pairs = [(group[i], group[i ^ step]) for group in Z_GROUPS for i in range(8)]
        sent = lax.ppermute(hot_part[half:].astype(jnp.bfloat16), "dp", pairs)
        hot_part = hot_part[:half] + sent.astype(jnp.float32)
    by_z = add_up(cold_pieces).astype(jnp.bfloat16).reshape(8, -1, model_width)
    by_z = lax.all_to_all(
        by_z, "dp", split_axis=0, concat_axis=0, tiled=True, axis_index_groups=Z_GROUPS
    )
    cold_sum = jnp.sum(by_z.astype(jnp.float32), axis=0)
    hot_sum = add_up(exchange([hot_part] * 4, "table", Y_GROUPS)).reshape(4, 1, 2, model_width)
    other = lax.ppermute(hot_sum, "table", shift(CORE_GROUPS, 1))
    ordered = jnp.where(
        core_at == 0,
        jnp.concatenate([hot_sum, other], axis=1),
        jnp.concatenate([other, hot_sum], axis=1),
    )
    return (layer_out, ordered.reshape(16, model_width), cold_sum)


def solution(mesh):
    placed = (
        P(),
        P("table", None),
        P(),
        P(),
        P(("table", "dp"), None),
        P(("table", "dp")),
        P(("table", "dp")),
        P(("table", "dp"), None),
        P(("table", "dp"), None),
    )
    return jax.shard_map(
        on_device,
        mesh=mesh,
        in_specs=placed,
        out_specs=(P(("table", "dp"), None), P("dp", None), P(("table", "dp"), None)),
        check_vma=False,
    )
```

```python
import jax
import jax.numpy as jnp
from jax import lax
from jax.experimental import pallas as pl
from jax.experimental.pallas import tpu as pltpu
from jax.sharding import PartitionSpec as P

HEAD = 128


EPS = 1e-06
BLOCK = 256
BACK = 1


def sigmoid(values):
    return 0.5 * jnp.tanh(0.5 * values) + 0.5


def mean_of(values):
    return jnp.mean(values, axis=-1, keepdims=True)


def dot_nn(a, b):
    return jnp.dot(a, b, preferred_element_type=jnp.float32)


def dot_nt(a, b):
    return lax.dot_general(a, b, (((1,), (1,)), ((), ())), preferred_element_type=jnp.float32)


def dot_tn(a, b):
    return lax.dot_general(a, b, (((0,), (0,)), ((), ())), preferred_element_type=jnp.float32)


def bring_kernel(after_ref, table_hbm, table_ref, sem):
    copy = pltpu.make_async_copy(table_hbm, table_ref, sem)
    copy.start()
    copy.wait()


def bring(table, after):
    vmem = pl.BlockSpec(memory_space=pltpu.VMEM)
    return pl.pallas_call(
        bring_kernel,
        out_shape=jax.ShapeDtypeStruct(table.shape, table.dtype),
        in_specs=[vmem, pl.BlockSpec(memory_space=pl.ANY)],
        out_specs=vmem,
        scratch_shapes=[pltpu.SemaphoreType.DMA],
        compiler_params=pltpu.CompilerParams(vmem_limit_bytes=4 * 1024 * 1024),
        cost_estimate=pl.CostEstimate(flops=0, bytes_accessed=2 * 10**6, transcendentals=0),
        name="bring",
    )(after, table)


def pick_kernel(wanted_ref, table_ref, rows_ref):
    takers, cap = wanted_ref.shape
    shard_rows, count = table_ref.shape[0], takers * cap
    wide = jnp.concatenate([wanted_ref[...]] * takers, axis=1)
    taker = lax.broadcasted_iota(jnp.int32, (takers, count), 0)
    lane = lax.broadcasted_iota(jnp.int32, (takers, count), 1)
    own = (lane >= taker * cap) & (lane < taker * cap + cap)
    flat = jnp.sum(jnp.where(own, wide, 0), axis=0, keepdims=True)
    pick = (lax.broadcasted_iota(jnp.int32, (shard_rows, count), 0) == flat).astype(jnp.bfloat16)
    rows_ref[...] = dot_tn(pick, table_ref[...]).astype(jnp.bfloat16)


def pick_rows(wanted, table):
    vmem = pl.BlockSpec(memory_space=pltpu.VMEM)
    return pl.pallas_call(
        pick_kernel,
        out_shape=jax.ShapeDtypeStruct((wanted.size, table.shape[1]), jnp.bfloat16),
        in_specs=[vmem] * 2,
        out_specs=vmem,
        compiler_params=pltpu.CompilerParams(vmem_limit_bytes=4 * 1024 * 1024),
        name="pick_rows",
    )(wanted, table)


def layer_kernel(
    ends_ref,
    source_ref,
    place_ref,
    fetched_hbm,
    hot_hbm,
    w_in_hbm,
    w_out_hbm,
    out_grad_hbm,
    layer_out_hbm,
    near_ref,
    far_ref,
    fetched_ref,
    hot_ref,
    w_in_ref,
    w_out_ref,
    out_grad_ref,
    layer_out_ref,
    rows_ref,
    normed_ref,
    rstd_ref,
    mixed_ref,
    slope_ref,
    weights_ref,
    dscore_ref,
    attended_ref,
    dvalue_ref,
    dkey_ref,
    dpre_ref,
    dnorm_ref,
    sems,
):
    tokens, width = rows_ref.shape
    hot_rows, slot_count = hot_ref.shape[0], fetched_ref.shape[0]
    inner = w_out_ref.shape[0]
    heads = inner // HEAD
    bf16, f32 = jnp.bfloat16, jnp.float32

    hot_copy = pltpu.make_async_copy(hot_hbm, hot_ref, sems.at[0])
    w_in_copy = pltpu.make_async_copy(w_in_hbm, w_in_ref, sems.at[1])
    w_out_copy = pltpu.make_async_copy(w_out_hbm, w_out_ref, sems.at[2])
    out_grad_copy = pltpu.make_async_copy(out_grad_hbm, out_grad_ref, sems.at[3])
    layer_out_copy = pltpu.make_async_copy(layer_out_ref, layer_out_hbm, sems.at[4])
    fetched_copy = pltpu.make_async_copy(fetched_hbm, fetched_ref, sems.at[5])
    for copy in (hot_copy, fetched_copy, w_in_copy, w_out_copy, out_grad_copy):
        copy.start()
    hot_copy.wait()

    for block in range(tokens // 256):
        at = pl.ds(block * 256, 256)
        source = source_ref[at, :]
        hot_pick = (source == lax.broadcasted_iota(jnp.int32, (256, hot_rows), 1)).astype(bf16)
        slot_pick = (
            source == lax.broadcasted_iota(jnp.int32, (256, slot_count), 1) + hot_rows
        ).astype(bf16)
        rows = dot_nn(hot_pick, hot_ref[...])
        if block == 0:
            fetched_copy.wait()
        rows = rows + dot_nn(slot_pick, fetched_ref[...])
        centered = rows - mean_of(rows)
        rstd = lax.rsqrt(mean_of(centered * centered) + EPS)
        rows_ref[at, :] = rows.astype(bf16)
        normed_ref[at, :] = (centered * rstd).astype(bf16)
        rstd_ref[at, :] = rstd

    w_in_copy.wait()

    for step in range(4 * inner // 256):
        at = pl.ds(step * 256, 256)
        pre = dot_nn(normed_ref[...], w_in_ref[:, at])
        sig = sigmoid(pre)
        act = pre * sig
        mixed_ref[:, at] = act.astype(bf16)
        slope_ref[:, at] = (sig + act * (1.0 - sig)).astype(bf16)

    def columns(part, head):
        return pl.ds(part * inner + head * HEAD, HEAD)

    for block in range(tokens // BLOCK):
        q_at = pl.ds(block * BLOCK, BLOCK)
        first = max(0, block - BACK)
        reach = (block + 1 - first) * BLOCK
        k_at = pl.ds(first * BLOCK, reach)
        position = lax.broadcasted_iota(jnp.int32, (BLOCK, 1), 0) + block * BLOCK
        begin = jnp.zeros((BLOCK, 1), jnp.int32)
        length = jnp.zeros((BLOCK, 1), jnp.int32)
        end = jnp.int32(0)
        for history in range(ends_ref.shape[1]):
            start = end
            end = ends_ref[0, history]
            inside = position >= start
            begin = jnp.where(inside, start, begin)
            length = jnp.where(inside, end - start, length)
        key_position = lax.broadcasted_iota(jnp.int32, (BLOCK, reach), 1) + first * BLOCK
        allowed = (key_position <= position) & (key_position >= begin)
        share = jnp.where(allowed, 1.0 / length.astype(f32), 0.0)
        for head in range(heads):
            scores = dot_nt(
                mixed_ref[q_at, columns(2, head)], mixed_ref[k_at, columns(3, head)]
            ) * (HEAD ** -0.5)
            sig = sigmoid(scores)
            act = scores * sig
            weights = (act * share).astype(bf16)
            weights_ref[head, q_at, :reach] = weights
            dscore_ref[head, q_at, :reach] = (
                (sig + act * (1.0 - sig)) * (share * (HEAD ** -0.5))
            ).astype(bf16)
            attended_ref[q_at, pl.ds(head * HEAD, HEAD)] = dot_nn(
                weights, mixed_ref[k_at, columns(1, head)]
            )

    w_out_copy.wait()
    out_grad_copy.wait()

    for block in range(tokens // 256):
        at = pl.ds(block * 256, 256)
        attended = attended_ref[at, :]
        centered = attended - mean_of(attended)
        rstd = lax.rsqrt(mean_of(centered * centered) + EPS)
        unit = centered * rstd
        gate = mixed_ref[at, :inner].astype(f32)
        merged = (unit * gate).astype(bf16)
        layer_out_ref[at, :] = (
            dot_nn(merged, w_out_ref[...]) + rows_ref[at, :].astype(f32)
        ).astype(bf16)
        dmerged = dot_nt(out_grad_ref[at, :], w_out_ref[...])
        dpre_ref[at, :inner] = (dmerged * unit * slope_ref[at, :inner].astype(f32)).astype(bf16)
        dunit = dmerged * gate
        attended_ref[at, :] = rstd * (dunit - mean_of(dunit) - unit * mean_of(dunit * unit))

    layer_out_copy.start()

    dvalue_ref[...] = jnp.zeros_like(dvalue_ref)
    dkey_ref[...] = jnp.zeros_like(dkey_ref)
    for block in range(tokens // BLOCK):
        q_at = pl.ds(block * BLOCK, BLOCK)
        first = max(0, block - BACK)
        reach = (block + 1 - first) * BLOCK
        k_at = pl.ds(first * BLOCK, reach)
        for head in range(heads):
            own = pl.ds(head * HEAD, HEAD)
            dattended = attended_ref[q_at, own].astype(bf16)
            dweights = dot_nt(dattended, mixed_ref[k_at, columns(1, head)])
            dscores = (dweights * dscore_ref[head, q_at, :reach].astype(f32)).astype(bf16)
            dquery = dot_nn(dscores, mixed_ref[k_at, columns(3, head)])
            dpre_ref[q_at, columns(2, head)] = (
                dquery * slope_ref[q_at, columns(2, head)].astype(f32)
            ).astype(bf16)
            dvalue_ref[k_at, own] += dot_tn(weights_ref[head, q_at, :reach], dattended)
            dkey_ref[k_at, own] += dot_tn(dscores, mixed_ref[q_at, columns(2, head)])
    values, keys = pl.ds(inner, inner), pl.ds(3 * inner, inner)
    dpre_ref[:, values] = (dvalue_ref[...] * slope_ref[:, values].astype(f32)).astype(bf16)
    dpre_ref[:, keys] = (dkey_ref[...] * slope_ref[:, keys].astype(f32)).astype(bf16)

    for step in range(width // 256):
        at = pl.ds(step * 256, 256)
        dnorm_ref[:, at] = dot_nt(dpre_ref[...], w_in_ref[at, :])

    for block in range(tokens // 64):
        at = pl.ds(block * 64, 64)
        rstd = rstd_ref[at, :]
        unit = normed_ref[at, :].astype(f32)
        dunit = dnorm_ref[at, :]
        grads = rstd * (dunit - mean_of(dunit) - unit * mean_of(dunit * unit))
        normed_ref[at, :] = (grads + out_grad_ref[at, :].astype(f32)).astype(bf16)

    half = near_ref.shape[0]
    for base, ref in ((half, far_ref), (0, near_ref)):
        pick = (
            lax.broadcasted_iota(jnp.int32, (half, tokens), 0) + base == place_ref[...]
        ).astype(bf16)
        for part in range(2):
            at = pl.ds(part * (width // 2), width // 2)
            ref[:, at] = dot_nn(pick, normed_ref[:, at]).astype(bf16)
    layer_out_copy.wait()


def layer(lengths, hot_table, fetched, w_in, w_out, out_grad, source, place):
    tokens, width = out_grad.shape
    inner = w_out.shape[0]
    heads = inner // HEAD
    half = (hot_table.shape[0] + fetched.shape[0]) // 2
    bf16, f32 = jnp.bfloat16, jnp.float32
    vmem = pl.BlockSpec(memory_space=pltpu.VMEM)
    hbm = pl.BlockSpec(memory_space=pl.ANY)
    reach = (BACK + 1) * BLOCK
    before = lax.iota(jnp.int32, lengths.shape[1])
    ends = jnp.sum(
        jnp.where(before[:, None] <= before[None, :], lengths.reshape(-1, 1), 0),
        axis=0,
        keepdims=True,
    )
    return pl.pallas_call(
        layer_kernel,
        out_shape=(
            jax.ShapeDtypeStruct((tokens, width), bf16),
            jax.ShapeDtypeStruct((half, width), bf16),
            jax.ShapeDtypeStruct((half, width), bf16),
        ),
        in_specs=[pl.BlockSpec(memory_space=pltpu.SMEM)] + [vmem] * 2 + [hbm] * 5,
        out_specs=(hbm, vmem, vmem),
        scratch_shapes=[
            pltpu.VMEM(fetched.shape, bf16),
            pltpu.VMEM(hot_table.shape, bf16),
            pltpu.VMEM(w_in.shape, bf16),
            pltpu.VMEM(w_out.shape, bf16),
            pltpu.VMEM((tokens, width), bf16),
            pltpu.VMEM((tokens, width), bf16),
            pltpu.VMEM((tokens, width), bf16),
            pltpu.VMEM((tokens, width), bf16),
            pltpu.VMEM((tokens, 1), f32),
            pltpu.VMEM((tokens, 4 * inner), bf16),
            pltpu.VMEM((tokens, 4 * inner), bf16),
            pltpu.VMEM((heads, tokens, reach), bf16),
            pltpu.VMEM((heads, tokens, reach), bf16),
            pltpu.VMEM((tokens, inner), f32),
            pltpu.VMEM((tokens, inner), f32),
            pltpu.VMEM((tokens, inner), f32),
            pltpu.VMEM((tokens, 4 * inner), bf16),
            pltpu.VMEM((tokens, width), f32),
            pltpu.SemaphoreType.DMA((6,)),
        ],
        compiler_params=pltpu.CompilerParams(vmem_limit_bytes=52 * 1024 * 1024),
        cost_estimate=pl.CostEstimate(flops=8 * 10**9, bytes_accessed=12 * 10**6, transcendentals=0),
        name="layer",
    )(ends, source, place, fetched, hot_table, w_in, w_out, out_grad)


def core_sums_kernel(near_ref, got_ref, *out_refs):
    slots = near_ref.shape[0] // 5
    hot = near_ref.shape[0] - slots
    for k in range(4):
        piece = pl.ds(k * slots // 4 + hot, slots // 4)
        out_refs[k][: slots // 4, :] = near_ref[piece, :]
        out_refs[k][slots // 4 :, :] = got_ref[piece, :]
    for k in range(4):
        piece = pl.ds(k * hot // 4, hot // 4)
        total = near_ref[piece, :].astype(jnp.float32) + got_ref[piece, :].astype(jnp.float32)
        out_refs[4 + k][...] = total.astype(jnp.bfloat16)


def core_sums(near, got):
    size, width = near.shape[0] // 5, near.shape[1]
    vmem = pl.BlockSpec(memory_space=pltpu.VMEM)
    out = pl.pallas_call(
        core_sums_kernel,
        out_shape=[jax.ShapeDtypeStruct((size // 2, width), jnp.bfloat16)] * 4
        + [jax.ShapeDtypeStruct((size, width), jnp.bfloat16)] * 4,
        in_specs=[vmem] * 2,
        out_specs=[vmem] * 8,
        compiler_params=pltpu.CompilerParams(vmem_limit_bytes=8 * 1024 * 1024),
        name="core_sums",
    )(near, got)
    return out[:4], out[4:]


def shard_sums_kernel(place_ref, own_ref, first_ref, second_ref, third_ref, *out_refs):
    rows = out_refs[0].shape[0]
    slots = jnp.concatenate(
        [own_ref[...], first_ref[...], second_ref[...], third_ref[...]], axis=0
    )
    for k, ref in enumerate(out_refs):
        pick = (
            lax.broadcasted_iota(jnp.int32, (rows, slots.shape[0]), 0) + k * rows == place_ref[...]
        ).astype(jnp.bfloat16)
        ref[...] = dot_nn(pick, slots).astype(jnp.bfloat16)


def shard_sums(place, pieces, shard_rows):
    width = pieces[0].shape[1]
    vmem = pl.BlockSpec(memory_space=pltpu.VMEM)
    return pl.pallas_call(
        shard_sums_kernel,
        out_shape=[jax.ShapeDtypeStruct((shard_rows // 4, width), jnp.bfloat16)] * 4,
        in_specs=[vmem] * 5,
        out_specs=[vmem] * 4,
        compiler_params=pltpu.CompilerParams(vmem_limit_bytes=4 * 1024 * 1024),
        name="shard_sums",
    )(place, *pieces)


def shift(groups, step):
    return [(g[i], g[(i + step) % len(g)]) for g in groups for i in range(len(g))]


CORE_GROUPS = [[2 * y, 2 * y + 1] for y in range(4)]
Y_GROUPS = [[2 * y + core for y in range(4)] for core in range(2)]
X_GROUPS = [[4 * z + x for x in range(4)] for z in range(8)]
Z_GROUPS = [[4 * z + x for z in range(8)] for x in range(4)]


def exchange(chunks, axis, groups):
    return [
        chunk if k == 0 else lax.ppermute(chunk, axis, shift(groups, k))
        for k, chunk in enumerate(chunks)
    ]


def add_up(pieces):
    here, back_1, back_2, back_3 = [piece.astype(jnp.float32) for piece in pieces]
    return (here + back_2) + (back_1 + back_3)


def on_device(
    hot_table, cold_table, w_in, w_out, seq_lengths, event_hot, event_index, cold_requests, out_grad
):
    table_count = lax.axis_size("table")
    cap_size = cold_requests.shape[1]
    slot_count = table_count * cap_size
    shard_rows = cold_table.shape[0]
    model_width = cold_table.shape[1]
    hot_rows = hot_table.shape[0]
    table_at, dp_at = lax.axis_index("table"), lax.axis_index("dp")
    y_at, core_at, x_at, z_at = table_at // 2, table_at % 2, dp_at % 4, dp_at // 4

    wanted = lax.all_to_all(cold_requests, "table", split_axis=0, concat_axis=0, tiled=True)
    fetched = lax.all_to_all(
        pick_rows(wanted, bring(cold_table, cold_requests)).reshape(table_count, cap_size, model_width),
        "table",
        split_axis=0,
        concat_axis=0,
        tiled=True,
    ).reshape(slot_count, model_width)
    wanted = wanted.reshape(slot_count)
    is_hot = event_hot == 1

    hot_dp, hot_t = event_index // 16, (event_index % 16) // 2
    z_step = (hot_dp // 4) ^ z_at
    hot_place = (
        (hot_t % 2 - core_at) % 2 * 320
        + (hot_dp % 4 - x_at) % 4 * 64
        + (z_step % 2 * 4 + z_step // 2 % 2 * 2 + z_step // 4) * 8
        + hot_t // 2 * 2
        + event_index % 2
    )
    slot_t = event_index // 16
    slot_place = (
        (slot_t % 2 - core_at) % 2 * 320
        + 256
        + (slot_t // 2 - y_at) % 4 * 16
        + event_index % 16
    )
    source = jnp.where(is_hot, event_index, event_index + hot_rows)
    place = jnp.where(is_hot, hot_place, slot_place)
    layer_out, near, far = layer(
        seq_lengths,
        hot_table,
        fetched,
        w_in,
        w_out,
        out_grad,
        source.reshape(-1, 1),
        place.reshape(1, -1),
    )
    got = lax.ppermute(far, "table", shift(CORE_GROUPS, 1))
    slot_chunks, hot_chunks = core_sums(near, got)
    pieces = exchange(slot_chunks, "table", Y_GROUPS)
    hot_part = add_up(exchange(hot_chunks, "dp", X_GROUPS))
    shard_place = (wanted // 16 % 4 - x_at) % 4 * 128 + wanted // 64 * 16 + wanted % 16
    back = (y_at - lax.iota(jnp.int32, 4)) % 4
    cores = (core_at + lax.iota(jnp.int32, 2)) % 2
    arriving = (back[:, None] * 2 + cores[None, :]).reshape(table_count)
    shard_place = shard_place.reshape(table_count, cap_size)[arriving].reshape(1, slot_count)
    cold_chunks = shard_sums(shard_place, pieces, shard_rows)
    cold_pieces = exchange(cold_chunks, "dp", X_GROUPS)

    for step in (1, 2, 4):
        half = hot_part.shape[0] // 2
        pairs = [(group[i], group[i ^ step]) for group in Z_GROUPS for i in range(8)]
        sent = lax.ppermute(hot_part[half:].astype(jnp.bfloat16), "dp", pairs)
        hot_part = hot_part[:half] + sent.astype(jnp.float32)
    by_z = add_up(cold_pieces).astype(jnp.bfloat16).reshape(8, -1, model_width)
    by_z = lax.all_to_all(
        by_z, "dp", split_axis=0, concat_axis=0, tiled=True, axis_index_groups=Z_GROUPS
    )
    cold_sum = jnp.sum(by_z.astype(jnp.float32), axis=0)
    hot_sum = add_up(exchange([hot_part] * 4, "table", Y_GROUPS)).reshape(4, 1, 2, model_width)
    other = lax.ppermute(hot_sum, "table", shift(CORE_GROUPS, 1))
    ordered = jnp.where(
        core_at == 0,
        jnp.concatenate([hot_sum, other], axis=1),
        jnp.concatenate([other, hot_sum], axis=1),
    )
    return (layer_out, ordered.reshape(16, model_width), cold_sum)


def solution(mesh):
    placed = (
        P(),
        P("table", None),
        P(),
        P(),
        P(("table", "dp"), None),
        P(("table", "dp")),
        P(("table", "dp")),
        P(("table", "dp"), None),
        P(("table", "dp"), None),
    )
    return jax.shard_map(
        on_device,
        mesh=mesh,
        in_specs=placed,
        out_specs=(P(("table", "dp"), None), P("dp", None), P(("table", "dp"), None)),
        check_vma=False,
    )
```
